32 devices in a mesh: dp: 2 (over x), row: 4 (over z), col: 4 (over y, core).
Axes of the slice: x: 2, y: 2, z: 4, core: 2. Of those that a mesh axis runs over, the one named last changes fastest.
Arguments:
- inputs: bfloat16 [2304, 4, 384], P(('dp', 'col'), 'row'), may hold values from -6 to 6
- cotangent: bfloat16 [2304, 4, 384], P(('dp', 'col'), 'row'), may hold values from -6 to 6
- slot_mask: int32 [8], replicated, may hold values from 0 to 1, as said below
- region_ids: int32 [24, 24], replicated, may hold values from 0 to 8, as said below
- offset_index: int32 [144, 144], replicated, may hold values from 0 to 528, as said below
- first_gain: float32 [768], P('row'), may hold values from 0.5 to 1.5
- first_shift: float32 [768], P('row'), may hold values from -1.75 to 1.75
- query_key_value: bfloat16 [384, 3, 4, 384], P('row', None, 'col'), may hold values from -0.21875 to 0.21875
- query_value_bias: float32 [2, 768], P(None, 'col'), may hold values from -3 to 3
- position_table: float32 [529, 24], P(None, 'col'), may hold values from -6 to 6
- output_weight: bfloat16 [384, 4, 384], P('col', 'row'), may hold values from -0.625 to 0.625
- output_bias: float32 [768], P('row'), may hold values from -1.75 to 1.75
- second_gain: float32 [768], P('row'), may hold values from 0.5 to 1.5
- second_shift: float32 [768], P('row'), may hold values from -1.75 to 1.75
- expand_weight: bfloat16 [768, 3072], P('row', 'col'), may hold values from -0.21875 to 0.21875
- expand_bias: float32 [3072], P('col'), may hold values from -1.75 to 1.75
- contract_weight: bfloat16 [1536, 4, 384], P('col', 'row'), may hold values from -0.109375 to 0.109375
- contract_bias: float32 [768], P('row'), may hold values from -1.75 to 1.75
Outputs:
- layer_output: bfloat16 [2304, 4, 384], P(('dp', 'col'), 'row')
- input_gradient: float32 [2304, 4, 384], P(('dp', 'col'), 'row')
- first_gain_gradient: float32 [768], P('row')
- first_shift_gradient: float32 [768], P('row')
- query_key_value_gradient: float32 [384, 3, 4, 384], P('row', None, 'col')
- query_value_bias_gradient: float32 [2, 768], P(None, 'col')
- position_table_gradient: float32 [529, 24], P(None, 'col')
- output_weight_gradient: float32 [384, 4, 384], P('col', 'row')
- output_bias_gradient: float32 [768], P('row')
- second_gain_gradient: float32 [768], P('row')
- second_shift_gradient: float32 [768], P('row')
- expand_weight_gradient: float32 [768, 3072], P('row', 'col')
- expand_bias_gradient: float32 [3072], P('col')
- contract_weight_gradient: float32 [1536, 4, 384], P('col', 'row')
- contract_bias_gradient: float32 [768], P('row')
The draws below stay inside these ranges and needn't reach their ends.
Inputs may be any that keep to these rules, and one draw needn't show every extreme that they name: `slot_mask`: 1 on the first slots and 0 on the rest; at least one slot of each kind. `region_ids`: 3 times a band of the token's row plus a band of its column; bands 0, 1, 2 cut at two drawn places along each side, each band non-empty. `offset_index`: a one-to-one relabelling of the offset between two window positions: equal offsets give equal entries, and every entry appears.
All inputs are finite; a program needn't handle non-finite values.
Results may differ from the reference program's by a relative error of at most 0.012.
Values may be sent and summed in bfloat16 or wider, within the bound.
No kernel may reach another device: no remote copies, remote signals or barrier semaphores. Data moves between devices by JAX's collectives and lax.ppermute only.
A program may use at most 128 MiB of HBM per device.

```python
import jax
import jax.numpy as jnp
from jax import lax

D = 768
HEADS = 24
FF = 3072
HEAD_DIM = 32
ROW_BLOCK = 192
COL_BLOCK = 192
SIDE = 24
WIN = 12
SHIFT = 6
REL = 529
IMAGES = 8
TOKENS = 4608
N_ROW = 4
N_COL = 4


def draw_slot_mask(key, part):
    filled = jax.random.randint(key, (), IMAGES // 2 + 1, IMAGES)
    return (jnp.arange(IMAGES, dtype=jnp.int32) < filled).astype(jnp.int32)


def band_of(key_low, key_high):
    places = jnp.arange(SIDE, dtype=jnp.int32)
    low_cut = jax.random.randint(key_low, (), 1, SIDE // 2 + 1)
    high_cut = jax.random.randint(key_high, (), SIDE // 2 + 1, SIDE)
    return (places >= low_cut).astype(jnp.int32) + (places >= high_cut).astype(jnp.int32)


def draw_region_ids(key, part):
    key_one, key_two, key_three, key_four = jax.random.split(key, 4)
    return 3 * band_of(key_one, key_two)[:, None] + band_of(key_three, key_four)[None, :]


def draw_offset_index(key, part):
    window_cells = jnp.arange(WIN * WIN, dtype=jnp.int32)
    row_pos = window_cells // WIN
    col_pos = window_cells % WIN
    offsets = (row_pos[:, None] - row_pos[None, :] + WIN - 1) * (2 * WIN - 1) + (col_pos[:, None] - col_pos[None, :] + WIN - 1)
    relabel = jax.random.permutation(key, (2 * WIN - 1) ** 2).astype(jnp.int32)
    return jnp.take(relabel, offsets)


def level_of(rng, shape, cuts, smallest, high):
    gain, own = 1.0, jax.random.fold_in(rng, 6)
    for dim, blocks in cuts:
        steps = jnp.exp(jax.random.uniform(jax.random.fold_in(own, dim), (blocks,), jnp.float32, smallest / len(cuts), high / len(cuts)))
        gain = gain * jnp.repeat(steps, shape[dim] // blocks).reshape([-1 if axis == dim else 1 for axis in range(len(shape))])
    return gain


def scatter_about(rng, extent, deviation, reach, shards=(), held_as=jnp.bfloat16):
    drawn = jax.random.normal(rng, extent, jnp.float32) * deviation
    if len(shards) > 0:
        drawn = level_of(rng, extent, shards, -0.22, 0.18) * drawn
    return jnp.clip(drawn, min=-reach, max=reach).astype(held_as)


def setup_inputs(seed: int = 0) -> dict:
    keys = jax.random.split(jax.random.key(seed), 19)
    inputs = scatter_about(keys[0], (TOKENS // 2, N_ROW, 2 * ROW_BLOCK), 1.0, 6.0, ((0, 8), (1, 4)))
    cotangent = scatter_about(keys[1], (TOKENS // 2, N_ROW, 2 * ROW_BLOCK), 1.0, 6.0, ((0, 8), (1, 4)))
    slot_mask = draw_slot_mask(jax.random.fold_in(keys[18], 71), 0)
    region_ids = draw_region_ids(jax.random.fold_in(keys[18], 71), 0)
    offset_index = draw_offset_index(jax.random.fold_in(keys[18], 71), 0)
    first_gain = jnp.clip(1.0 + 0.1 * jax.random.normal(keys[5], (D,), jnp.float32), 0.5, 1.5)
    first_shift = scatter_about(keys[6], (D,), 0.3, 1.75, ((0, 4),), jnp.float32)
    query_key_value = scatter_about(keys[7], (D // 2, 3, N_COL, 2 * COL_BLOCK), D ** -0.5, 0.21875, ((0, 4), (2, 4)))
    query_value_bias = scatter_about(keys[8], (2, D), 0.5, 3.0, ((1, 4),), jnp.float32)
    position_table = scatter_about(keys[9], (REL, HEADS), 1.0, 6.0, ((1, 4),), jnp.float32)
    output_weight = scatter_about(keys[10], (D // 2, N_ROW, 2 * ROW_BLOCK), (D // 8) ** -0.5, 0.625, ((0, 4), (1, 4)))
    output_bias = scatter_about(keys[11], (D,), 0.3, 1.75, ((0, 4),), jnp.float32)
    second_gain = jnp.clip(1.0 + 0.1 * jax.random.normal(keys[12], (D,), jnp.float32), 0.5, 1.5)
    second_shift = scatter_about(keys[13], (D,), 0.3, 1.75, ((0, 4),), jnp.float32)
    expand_weight = scatter_about(keys[14], (D, FF), D ** -0.5, 0.21875, ((0, 4), (1, 4)))
    expand_bias = scatter_about(keys[15], (FF,), 0.3, 1.75, ((0, 4),), jnp.float32)
    contract_weight = scatter_about(keys[16], (FF // 2, N_ROW, 2 * ROW_BLOCK), FF ** -0.5, 0.109375, ((0, 4), (1, 4)))
    contract_bias = scatter_about(keys[17], (D,), 0.3, 1.75, ((0, 4),), jnp.float32)
    return {"inputs": inputs, "cotangent": cotangent, "slot_mask": slot_mask, "region_ids": region_ids, "offset_index": offset_index, "first_gain": first_gain, "first_shift": first_shift, "query_key_value": query_key_value, "query_value_bias": query_value_bias, "position_table": position_table, "output_weight": output_weight, "output_bias": output_bias, "second_gain": second_gain, "second_shift": second_shift, "expand_weight": expand_weight, "expand_bias": expand_bias, "contract_weight": contract_weight, "contract_bias": contract_bias}


NORM_EPS = 1e-05
MASK_FILL = -100.0
HIGHEST = lax.Precision.HIGHEST

@jax.custom_vjp
def low(v):
    return lax.optimization_barrier(v.astype(jnp.bfloat16)).astype(jnp.float32)

@jax.custom_vjp
def low_back(v):
    return v

def low_keep(v):
    return (low(v), None)

def low_pass(kept, grad):
    return (grad,)

def back_keep(v):
    return (v, None)

def back_low(kept, grad):
    return (low(grad),)
low.defvjp(low_keep, low_pass)
low_back.defvjp(back_keep, back_low)

def unpair_whole(paired):
    halves, blocks, doubled = paired.shape
    single = doubled // 2
    return paired.reshape(halves, blocks, 2, single).transpose(0, 2, 1, 3).reshape(halves * 2, blocks * single)

def pair_whole(matrix, blocks):
    count, columns = matrix.shape
    single = columns // blocks
    return matrix.reshape(count // 2, 2, blocks, single).transpose(0, 2, 1, 3).reshape(count // 2, blocks, 2 * single)

def unpair_joined(paired):
    halves, parts, blocks, doubled = paired.shape
    single = doubled // 2
    return paired.reshape(halves, parts, blocks, 2, single).transpose(0, 3, 1, 2, 4).reshape(halves * 2, parts, blocks * single)

def pair_joined(joined, blocks):
    count, parts, columns = joined.shape
    single = columns // blocks
    return joined.reshape(count // 2, 2, parts, blocks, single).transpose(0, 2, 3, 1, 4).reshape(count // 2, parts, blocks, 2 * single)

def layer_norm(values, norm_gain, norm_shift):
    centre = values - lax.optimization_barrier(jnp.mean(values, -1, keepdims=True))
    spread = lax.optimization_barrier(jnp.mean(jnp.square(centre), -1, keepdims=True))
    return centre * lax.rsqrt(spread + NORM_EPS) * norm_gain + norm_shift

def to_windows(source, head_count):
    images = source.shape[0] // (SIDE * SIDE)
    blocks = SIDE // WIN
    shaped = source.reshape(images, SIDE, SIDE, head_count, HEAD_DIM)
    shaped = jnp.roll(shaped, (-SHIFT, -SHIFT), axis=(1, 2))
    shaped = shaped.reshape(images, blocks, WIN, blocks, WIN, head_count, HEAD_DIM)
    shaped = shaped.transpose(0, 1, 3, 5, 2, 4, 6)
    return shaped.reshape(images * blocks * blocks, head_count, WIN * WIN, HEAD_DIM)

def from_windows(windowed, head_count):
    blocks = SIDE // WIN
    images = windowed.shape[0] // (blocks * blocks)
    shaped = windowed.reshape(images, blocks, blocks, head_count, WIN, WIN, HEAD_DIM)
    shaped = shaped.transpose(0, 1, 4, 2, 5, 3, 6).reshape(images, SIDE, SIDE, head_count, HEAD_DIM)
    shaped = jnp.roll(shaped, (SHIFT, SHIFT), axis=(1, 2))
    return shaped.reshape(images * SIDE * SIDE, head_count * HEAD_DIM)

def region_mask(region_ids):
    blocks = SIDE // WIN
    labels = region_ids.reshape(blocks, WIN, blocks, WIN).transpose(0, 2, 1, 3).reshape(blocks * blocks, WIN * WIN)
    return jnp.where(labels[:, :, None] == labels[:, None, :], 0.0, MASK_FILL).astype(jnp.float32)

def forward(inputs, first_gain, first_shift, query_key_value, query_value_bias, position_table, output_weight, output_bias, second_gain, second_shift, expand_weight, expand_bias, contract_weight, contract_bias, offset_index, mask_block):
    head_count = position_table.shape[1]
    normed_one = low(layer_norm(inputs, first_gain, first_shift))
    projected = jnp.einsum('td,dsc->tsc', normed_one, query_key_value, precision=HIGHEST)
    bias_rows = jnp.stack([query_value_bias[0], jnp.zeros_like(query_value_bias[0]), query_value_bias[1]])
    projected = low_back(projected + bias_rows[None])
    queries = to_windows(low(projected[:, 0] * HEAD_DIM ** (-0.5)), head_count)
    keys_win = to_windows(low(projected[:, 1]), head_count)
    values_win = to_windows(low(projected[:, 2]), head_count)
    images = queries.shape[0] // mask_block.shape[0]
    bias_block = jnp.take(position_table, offset_index, axis=0).transpose(2, 0, 1)
    masks = jnp.tile(mask_block, (images, 1, 1))
    scores = jnp.einsum('nhid,nhjd->nhij', queries, keys_win, precision=HIGHEST) + bias_block[None] + masks[:, None]
    probs = jax.nn.softmax(low_back(scores), axis=-1)
    attended = jnp.einsum('nhij,nhjd->nhid', low(probs), values_win, precision=HIGHEST)
    attended = low_back(low(from_windows(attended, head_count)))
    residual_mid = inputs + low_back(jnp.dot(attended, output_weight, precision=HIGHEST) + output_bias)
    normed_two = low(layer_norm(residual_mid, second_gain, second_shift))
    pre_act = low_back(jnp.dot(normed_two, expand_weight, precision=HIGHEST) + expand_bias)
    hidden = low(jax.nn.gelu(pre_act, approximate=False))
    return residual_mid + jnp.dot(hidden, contract_weight, precision=HIGHEST) + contract_bias

def reference(inputs, cotangent, slot_mask, region_ids, offset_index, first_gain, first_shift, query_key_value, query_value_bias, position_table, output_weight, output_bias, second_gain, second_shift, expand_weight, expand_bias, contract_weight, contract_bias):
    inputs_rows = unpair_whole(inputs)
    cotangent_rows = unpair_whole(cotangent)
    joined_plain = unpair_joined(query_key_value)
    output_plain = unpair_whole(output_weight)
    contract_plain = unpair_whole(contract_weight)
    params = tuple((member.astype(jnp.float32) for member in (first_gain, first_shift, joined_plain, query_value_bias, position_table, output_plain, output_bias, second_gain, second_shift, expand_weight, expand_bias, contract_plain, contract_bias)))
    mask_block = region_mask(region_ids)
    group_tokens = N_ROW * SIDE * SIDE
    groups = IMAGES // N_ROW
    token_flag = jnp.repeat(slot_mask, SIDE * SIDE).astype(jnp.float32)

    def forward_group(token_rows, *weights):
        return forward(token_rows, *weights, offset_index, mask_block)

    def step_group(running, member_rows):
        rows_in, rows_cot, rows_flag = member_rows
        result, pullback = jax.vjp(forward_group, rows_in.astype(jnp.float32), *params)
        gradients = pullback(rows_cot.astype(jnp.float32) * rows_flag[:, None])
        running = tuple((total + extra for total, extra in zip(running, gradients[1:])))
        return (running, (result.astype(jnp.bfloat16), gradients[0]))
    initial = tuple((jnp.zeros_like(member) for member in params))
    totals, (outputs, input_grads) = lax.scan(step_group, initial, (inputs_rows.reshape(groups, group_tokens, D), cotangent_rows.reshape(groups, group_tokens, D), token_flag.reshape(groups, group_tokens)))
    layer_output = pair_whole(outputs.reshape(TOKENS, D), N_ROW)
    input_gradient = pair_whole(input_grads.reshape(TOKENS, D), N_ROW)
    joined_grad = pair_joined(totals[2], N_COL)
    output_grad = pair_whole(totals[5], N_ROW)
    contract_grad = pair_whole(totals[11], N_ROW)
    return (layer_output, input_gradient, totals[0], totals[1], joined_grad, totals[3], totals[4], output_grad, totals[6], totals[7], totals[8], totals[9], totals[10], contract_grad, totals[12])
```

```python
import jax
import jax.numpy as jnp
from jax import lax
from jax.experimental import pallas as pl
from jax.experimental.pallas import tpu as pltpu
from jax.sharding import PartitionSpec as P

HEAD_DIM = 32
SIDE = 24
WIN = 12
SHIFT = 6
REL = 529
CELLS = WIN * WIN
NORM_EPS = 1e-05
MASK_FILL = -100.0
BF = jnp.bfloat16
F32 = jnp.float32
NT = (((1,), (1,)), ((), ()))
TN = (((0,), (0,)), ((), ()))
BLOCK = 192
WIDTH = 768
HALF = 384
GROUP = 4
TOKENS = GROUP * CELLS
HEADS = BLOCK // HEAD_DIM
ROOT_HALF = 0.7071067811865476
ROOT_TWO_PI_INV = 0.3989422804014327


def dot(a, b):
    return jnp.dot(a, b, preferred_element_type=F32)


def dot_nt(a, b):
    return lax.dot_general(a, b, NT, preferred_element_type=F32)


def dot_tn(a, b):
    return lax.dot_general(a, b, TN, preferred_element_type=F32)


def iota(shape, dim):
    return lax.broadcasted_iota(jnp.int32, shape, dim)


def aligned(value, step):
    return pl.multiple_of(value, step)


def run(kernel, outs, scratch, ids, *arrays):
    vmem = pl.BlockSpec(memory_space=pltpu.VMEM)
    return pl.pallas_call(
        kernel,
        out_shape=[jax.ShapeDtypeStruct(shape, dtype) for shape, dtype in outs],
        in_specs=[pl.BlockSpec(memory_space=pltpu.SMEM)] + [vmem] * len(arrays),
        out_specs=[vmem] * len(outs),
        scratch_shapes=[pltpu.VMEM(shape, dtype) for shape, dtype in scratch],
        compiler_params=pltpu.CompilerParams(vmem_limit_bytes=40 * 1024 * 1024),
        name=kernel.__name__,
    )(ids, *arrays)


def place(window, position):
    row = (position * 171) >> 11
    col = position - row * WIN
    row = row + (window // 2) * WIN + SHIFT
    col = col + (window % 2) * WIN + SHIFT
    row = jnp.where(row >= SIDE, row - SIDE, row)
    col = jnp.where(col >= SIDE, col - SIDE, col)
    token = row * SIDE + col
    return token >> 1, token & 1


def order_kernel(ids, paired, *outs):
    z = ids[1]
    count = paired.shape[0]
    even = paired[:, :BLOCK]
    odd = paired[:, BLOCK:]
    for s in range(GROUP):
        half, parity = place((z + s) % GROUP, iota((CELLS, count), 0))
        hit = half == iota((CELLS, count), 1)
        pick_even = jnp.where(hit & (parity == 0), 1.0, 0.0).astype(BF)
        pick_odd = jnp.where(hit & (parity == 1), 1.0, 0.0).astype(BF)
        outs[s][...] = (dot(pick_even, even) + dot(pick_odd, odd)).astype(BF)


def restore_halves(ids, pieces):
    z = ids[1]
    count = SIDE * SIDE // 2
    even = odd = None
    for s in range(GROUP):
        half, parity = place((z + s) % GROUP, iota((count, CELLS), 1))
        hit = half == iota((count, CELLS), 0)
        pick_even = jnp.where(hit & (parity == 0), 1.0, 0.0).astype(BF)
        pick_odd = jnp.where(hit & (parity == 1), 1.0, 0.0).astype(BF)
        piece = pieces[s][...]
        more_even = dot(pick_even, piece)
        more_odd = dot(pick_odd, piece)
        even = more_even if even is None else even + more_even
        odd = more_odd if odd is None else odd + more_odd
    return even, odd


def restore_kernel(ids, a, b, c, d, out):
    even, odd = restore_halves(ids, (a, b, c, d))
    out[:, :BLOCK] = even.astype(BF)
    out[:, BLOCK:] = odd.astype(BF)


def restore_wide_kernel(ids, a, b, c, d, out, whole):
    even, odd = restore_halves(ids, (a, b, c, d))
    whole[:, :BLOCK] = even
    whole[:, BLOCK:] = odd
    count = whole.shape[0]
    for k in range(3):
        out[pl.ds(k, count, stride=3), :] = whole[:, k * 128 : (k + 1) * 128]


def pair_picks(rows):
    low = iota((rows, rows // 2), 0)
    high = iota((rows, rows // 2), 1)
    pick_even = jnp.where(low == 2 * high, 1.0, 0.0).astype(BF)
    pick_odd = jnp.where(low == 2 * high + 1, 1.0, 0.0).astype(BF)
    return pick_even, pick_odd


def hidden_perm():
    natural = iota((WIDTH, WIDTH), 0)
    split = iota((WIDTH, WIDTH), 1)
    wanted = jnp.where(split < HALF, 2 * split, 2 * split - (WIDTH - 1))
    return jnp.where(natural == wanted, 1.0, 0.0).astype(BF)


def join_halves(ids, own, mine, other, held, rows, where=()):
    x = ids[0]
    for s in range(GROUP):
        if s == 0:
            held[(s, *where)] = own[...]
        else:
            held[(s, *where, pl.ds(aligned(x * rows, 16), rows), slice(None))] = mine[s - 1][...]
            held[(s, *where, pl.ds(aligned((1 - x) * rows, 16), rows), slice(None))] = other[s - 1][...]


def qkv_weights_kernel(ids, own, m1, m2, m3, o1, o2, o3, out, held):
    pick_even, pick_odd = pair_picks(BLOCK)
    for part in range(3):
        join_halves(
            ids, own.at[part], [m.at[part] for m in (m1, m2, m3)], [o.at[part] for o in (o1, o2, o3)],
            held, BLOCK // 4, (part,),
        )
    for s in range(GROUP):
        for part in range(3):
            out[part, s * BLOCK : (s + 1) * BLOCK, :] = (
                dot(pick_even, held[s, part, :, :BLOCK]) + dot(pick_odd, held[s, part, :, BLOCK:])
            ).astype(BF)


def out_weights_kernel(ids, own, m1, m2, m3, o1, o2, o3, out, held):
    pick_even, pick_odd = pair_picks(BLOCK)
    join_halves(ids, own, (m1, m2, m3), (o1, o2, o3), held, BLOCK // 4)
    for s in range(GROUP):
        out[:, s * BLOCK : (s + 1) * BLOCK] = (
            dot(pick_even, held[s, :, :BLOCK]) + dot(pick_odd, held[s, :, BLOCK:])
        ).astype(BF)


def expand_weights_kernel(ids, own, m1, m2, m3, o1, o2, o3, out, held):
    perm = hidden_perm()
    join_halves(ids, own, (m1, m2, m3), (o1, o2, o3), held, BLOCK // 2)
    for s in range(GROUP):
        out[s * BLOCK : (s + 1) * BLOCK, :] = dot(held[s], perm).astype(BF)


def contract_weights_kernel(ids, own, m1, m2, m3, o1, o2, o3, out, held):
    join_halves(ids, own, (m1, m2, m3), (o1, o2, o3), held, HALF // 2)
    for s in range(GROUP):
        for q in range(2):
            out[q * HALF : (q + 1) * HALF, s * BLOCK : (s + 1) * BLOCK] = held[s, :, q * BLOCK : (q + 1) * BLOCK]


def entry_hits(offset, index):
    row = offset[pl.ds(index, 1), :]
    return jnp.where(iota((REL, CELLS), 0) == row, 1.0, 0.0).astype(BF)


def bias_kernel(ids, table, offset, labels, labels_t, out, parts, strips, mask):
    z = ids[1]
    parts[...] = jnp.zeros(parts.shape, F32)
    whole = table[...]
    high = whole.astype(BF).astype(F32)
    rest = whole - high
    middle = rest.astype(BF).astype(F32)
    parts[0:HEADS, :] = high
    parts[8 : 8 + HEADS, :] = middle
    parts[16 : 16 + HEADS, :] = rest - middle
    split = parts[...].astype(BF)
    row_label = labels[pl.ds(z, 1), :]
    col_label = jnp.sum(jnp.where(iota((CELLS, GROUP), 1) == z, labels_t[...], 0), axis=1, keepdims=True)
    mask[...] = jnp.where(row_label == col_label, 0.0, MASK_FILL)
    for c in range(WIN):
        upper = dot(split, entry_hits(offset, (WIN - 1) * WIN + c))
        lower = dot(split, entry_hits(offset, c))
        strips[c, :, 0:CELLS] = upper[0:8] + upper[8:16] + upper[16:24]
        strips[c, :, CELLS : CELLS + (WIN - 1) * WIN] = (lower[0:8] + lower[8:16] + lower[16:24])[:, WIN:]
    for h in range(HEADS):
        strip = strips[:, h, :]
        for r in range(WIN):
            begin = (WIN - 1 - r) * WIN
            out[h, r * WIN : (r + 1) * WIN, :] = (
                strip[:, begin : begin + CELLS] + mask[r * WIN : (r + 1) * WIN, :]
            )


def table_kernel(ids, grads, offset, out, strips, wide):
    for h in range(HEADS):
        wide[...] = jnp.zeros(wide.shape, F32)
        for r in range(WIN):
            begin = (WIN - 1 - r) * WIN
            wide[:, begin : begin + CELLS] += grads[h, r * WIN : (r + 1) * WIN, :]
        strips[:, h, :] = wide[...]
    total = jnp.zeros((16, REL), F32)
    for c in range(WIN):
        upper = strips[c, :, 0:CELLS]
        lower = jnp.concatenate(
            [jnp.zeros((8, WIN), F32), strips[c, :, CELLS : CELLS + (WIN - 1) * WIN]], axis=1
        )
        for index, piece in (((WIN - 1) * WIN + c, upper), (c, lower)):
            high = piece.astype(BF).astype(F32)
            both = jnp.concatenate([high, piece - high], axis=0).astype(BF)
            total = total + dot(both, entry_hits_t(offset, index))
    out[...] = total[0:8] + total[8:16]


def entry_hits_t(offset, index):
    hits = entry_hits(offset, index)
    return hits.T


def norm_stats(values):
    centre = jnp.mean(values, axis=-1, keepdims=True)
    moved = values - centre
    inverse = lax.rsqrt(jnp.mean(moved * moved, axis=-1, keepdims=True) + NORM_EPS)
    return moved * inverse, inverse


def wide_vector(vectors, row):
    return jnp.concatenate([v[row : row + 1, :] for v in vectors], axis=1)


def attend_kernel(ids, *refs):
    pieces = refs[0:16]
    vectors = refs[16:20]
    weights, head_bias, bias = refs[20:23]
    tokens, normed, queries, keys, values, probs, attended = refs[23:30]
    gain = wide_vector(vectors, 0)
    shift = wide_vector(vectors, 1)
    for j in range(GROUP):
        for s in range(GROUP):
            tokens[j * CELLS : (j + 1) * CELLS, s * BLOCK : (s + 1) * BLOCK] = pieces[j * GROUP + s][...]

    @pl.loop(0, GROUP)
    def _(w):
        rows = pl.ds(aligned(w * CELLS, 16), CELLS)
        scaled, _ = norm_stats(tokens[rows, :].astype(F32))
        normed[rows, :] = (scaled * gain + shift).astype(BF)

    scale = float(HEAD_DIM) ** (-0.5)
    whole = normed[...]
    queries[...] = ((dot(whole, weights[0]) + head_bias[0:1, :]) * scale).astype(BF)
    keys[...] = dot(whole, weights[1]).astype(BF)
    values[...] = (dot(whole, weights[2]) + head_bias[1:2, :]).astype(BF)
    lane_head = iota((CELLS, BLOCK), 1) // HEAD_DIM

    for w in range(GROUP):
        rows = pl.ds(w * CELLS, CELLS)
        query = queries[rows, :]
        key = keys[rows, :]
        value = values[rows, :]
        total = jnp.zeros((CELLS, BLOCK), F32)
        for h in range(HEADS):
            own = lane_head == h
            scores = dot_nt(jnp.where(own, query, jnp.zeros_like(query)), key) + bias[h]
            powers = jnp.exp(scores - jnp.max(scores, axis=-1, keepdims=True))
            share = (powers / jnp.sum(powers, axis=-1, keepdims=True)).astype(BF)
            probs[w * HEADS + h] = share
            total = total + dot(share, jnp.where(own, value, jnp.zeros_like(value)))
        attended[(w & 1) * CELLS : (w & 1) * CELLS + CELLS, (w >> 1) * BLOCK : (w >> 1) * BLOCK + BLOCK] = (
            total.astype(BF)
        )


def expand_kernel(ids, *refs):
    tokens = refs[0]
    attended = refs[1:5]
    out_weights = refs[5:9]
    vectors = refs[9:13]
    weights, hidden_bias = refs[13:15]
    middle, normed, hidden, slope = refs[15:19]
    joined, square = refs[19:21]
    for j in range(GROUP):
        square[j * BLOCK : (j + 1) * BLOCK, :] = out_weights[j][...]
        for i in range(GROUP):
            k = i ^ j
            joined[i * CELLS : (i + 1) * CELLS, j * BLOCK : (j + 1) * BLOCK] = attended[j][
                (k & 1) * CELLS : (k & 1) * CELLS + CELLS, (k >> 1) * BLOCK : (k >> 1) * BLOCK + BLOCK
            ]
    out_bias = wide_vector(vectors, 2)
    gain = wide_vector(vectors, 3)
    shift = wide_vector(vectors, 4)

    @pl.loop(0, 2)
    def _(t):
        rows = pl.ds(aligned(t * (TOKENS // 2), 16), TOKENS // 2)
        mid = tokens[rows, :].astype(F32) + dot(joined[rows, :], square[...]) + out_bias
        middle[rows, :] = mid
        scaled, _ = norm_stats(mid)
        second = (scaled * gain + shift).astype(BF)
        normed[rows, :] = second
        pre = dot(second, weights[...]) + hidden_bias[...]
        bell = 0.5 * (1.0 + lax.erf(pre * ROOT_HALF))
        hidden[rows, :] = (pre * bell).astype(BF)
        slope[rows, :] = bell + pre * (ROOT_TWO_PI_INV * jnp.exp(-0.5 * pre * pre))


def upstream_kernel(ids, slots, *refs):
    pieces = refs[0:16]
    out = refs[16]
    base = ids[3] * GROUP
    for j in range(GROUP):
        flag = slots[base + (ids[2] ^ j)] != 0
        for s in range(GROUP):
            piece = pieces[j * GROUP + s][...].astype(F32)
            out[j * CELLS : (j + 1) * CELLS, s * BLOCK : (s + 1) * BLOCK] = jnp.where(
                flag, piece, jnp.zeros_like(piece)
            ).astype(BF)


def split_slots(product, keep, send):
    keep[0:CELLS, :] = product[0:CELLS].astype(keep.dtype)
    keep[CELLS:, :] = product[2 * CELLS : 3 * CELLS].astype(keep.dtype)
    send[0:CELLS, :] = product[CELLS : 2 * CELLS].astype(send.dtype)
    send[CELLS:, :] = product[3 * CELLS :].astype(send.dtype)


def hidden_back_kernel(ids, upstream, contract, slope, expand, pre_grad, keep, send):
    pre_grad[...] = (dot_nt(upstream[...], contract[...]) * slope[...]).astype(BF)
    split_slots(dot_nt(pre_grad[...], expand[...]), keep, send)


def hidden_grads_kernel(
    ids, upstream, hidden, normed, pre_grad, contract,
    keep_c, send_c, keep_e, send_e, keep_out, send_out, sums, whole_c, whole_e,
):
    x = ids[0]
    up = upstream[...]
    for q in range(2):
        block = dot_tn(hidden[:, q * HALF : (q + 1) * HALF], up).astype(BF)
        for s in range(GROUP):
            whole_c[s, :, q * BLOCK : (q + 1) * BLOCK] = block[:, s * BLOCK : (s + 1) * BLOCK]
    rows = HALF // 2
    for s in range(GROUP):
        keep_c[s] = whole_c[s, pl.ds(aligned(x * rows, 16), rows), :]
        send_c[s] = whole_c[s, pl.ds(aligned((1 - x) * rows, 16), rows), :]
    mixed = dot_tn(normed[...], pre_grad[...]).astype(BF)
    whole_e[...] = dot_nt(mixed, hidden_perm()).astype(BF)
    rows = BLOCK // 2
    for s in range(GROUP):
        keep_e[s] = whole_e[pl.ds(aligned(s * BLOCK + x * rows, 16), rows), :]
        send_e[s] = whole_e[pl.ds(aligned(s * BLOCK + (1 - x) * rows, 16), rows), :]
    split_slots(dot(hidden[...], contract[...]), keep_out, send_out)
    sums[...] = jnp.zeros(sums.shape, F32)
    sums[0:1, :] = jnp.sum(pre_grad[...].astype(F32), axis=0, keepdims=True)
    sums[1:2, :] = jnp.sum(upstream[0:CELLS, :].astype(F32), axis=0, keepdims=True)


def attend_back_kernel(ids, *refs):
    even_total, odd_total, middle, upstream = refs[0:4]
    vectors = refs[4:8]
    out_weights, queries, keys, values, probs, weights = refs[8:14]
    own_mid, mid_low, joined, bias_grad, keep, send, sums = refs[14:21]
    attended_grad = refs[21]
    gain = wide_vector(vectors, 3)
    sums[...] = jnp.zeros(sums.shape, F32)
    for w in range(GROUP):
        rows = pl.ds(w * CELLS, CELLS)
        source = (even_total, odd_total)[w & 1]
        grad = source[(w >> 1) * CELLS : (w >> 1) * CELLS + CELLS, :].astype(F32)
        scaled, inverse = norm_stats(middle[rows, :])
        e = grad * gain
        part = e - jnp.mean(e, axis=-1, keepdims=True) - scaled * jnp.mean(e * scaled, axis=-1, keepdims=True)
        mid = upstream[rows, :].astype(F32) + inverse * part
        low = mid.astype(BF)
        mid_low[rows, :] = low
        if w == 0:
            own_mid[...] = mid
            sums[0:1, :] = jnp.sum(low.astype(F32), axis=0, keepdims=True)
            sums[1:2, :] = jnp.sum(grad * scaled, axis=0, keepdims=True)
            sums[2:3, :] = jnp.sum(grad, axis=0, keepdims=True)
    attended_grad[...] = dot_nt(mid_low[...], out_weights[...]).astype(BF)
    lane_head = iota((CELLS, BLOCK), 1) // HEAD_DIM
    scale = float(HEAD_DIM) ** (-0.5)
    for w in range(GROUP):
        rows = pl.ds(w * CELLS, CELLS)
        query = queries[rows, :]
        key = keys[rows, :]
        value = values[rows, :]
        grad = attended_grad[rows, :]
        query_grad = jnp.zeros((CELLS, BLOCK), F32)
        key_grad = jnp.zeros((CELLS, BLOCK), F32)
        value_grad = jnp.zeros((CELLS, BLOCK), F32)
        for h in range(HEADS):
            own = lane_head == h
            zero = jnp.zeros_like(query)
            own_grad = jnp.where(own, grad, zero)
            share = probs[w * HEADS + h]
            value_grad = value_grad + dot_tn(share, own_grad)
            prob_grad = dot_nt(own_grad, value)
            wide = share.astype(F32)
            product = wide * prob_grad
            score = (product - wide * jnp.sum(product, axis=-1, keepdims=True)).astype(BF)
            query_grad = query_grad + dot(score, jnp.where(own, key, zero))
            key_grad = key_grad + dot_tn(score, jnp.where(own, query, zero))
            if w == 0:
                bias_grad[h] = score.astype(F32)
            else:
                bias_grad[h] += score.astype(F32)
        joined[0, rows, :] = (query_grad * scale).astype(BF)
        joined[1, rows, :] = key_grad.astype(BF)
        joined[2, rows, :] = value_grad.astype(BF)
    product = dot_nt(joined[0], weights[0]) + dot_nt(joined[1], weights[1]) + dot_nt(joined[2], weights[2])
    split_slots(product, keep, send)


def joined_grads_kernel(
    ids, normed, joined, attended, mid_low, tokens, keep, send,
    keep_q, send_q, keep_o, send_o, sums, whole_q, whole_o,
):
    x = ids[0]
    whole = normed[...]
    picks = pair_picks(BLOCK)
    for part in range(3):
        natural = dot_tn(whole, joined[part]).astype(BF)
        for s in range(GROUP):
            for q in range(2):
                whole_q[part, s * (BLOCK // 2) : (s + 1) * (BLOCK // 2), q * BLOCK : (q + 1) * BLOCK] = dot_tn(
                    picks[q], natural[s * BLOCK : (s + 1) * BLOCK]
                ).astype(BF)
    rows = BLOCK // 4
    for part in range(3):
        for s in range(GROUP):
            begin = s * (BLOCK // 2)
            keep_q[s, part] = whole_q[part, pl.ds(aligned(begin + x * rows, 16), rows), :]
            send_q[s, part] = whole_q[part, pl.ds(aligned(begin + (1 - x) * rows, 16), rows), :]
    low = mid_low[...]
    total = None
    for k in range(2):
        left = attended[:, k * BLOCK : (k + 1) * BLOCK]
        product = dot_tn(left, low[2 * k * CELLS : (2 * k + 2) * CELLS])
        total = product if total is None else total + product
    wide = total.astype(BF)
    for q in range(2):
        lines = dot_tn(picks[q], wide).astype(BF)
        for s in range(GROUP):
            whole_o[s, :, q * BLOCK : (q + 1) * BLOCK] = lines[:, s * BLOCK : (s + 1) * BLOCK]
    for s in range(GROUP):
        keep_o[s] = whole_o[s, pl.ds(aligned(x * rows, 16), rows), :]
        send_o[s] = whole_o[s, pl.ds(aligned((1 - x) * rows, 16), rows), :]
    sums[...] = jnp.zeros(sums.shape, F32)
    gains = shifts = None
    for w in range(GROUP):
        source = (keep, send)[w & 1]
        grad = source[(w >> 1) * CELLS : (w >> 1) * CELLS + CELLS, :].astype(F32)
        scaled, _ = norm_stats(tokens[w * CELLS : (w + 1) * CELLS, :].astype(F32))
        more_gains = jnp.sum(grad * scaled, axis=0, keepdims=True)
        more_shifts = jnp.sum(grad, axis=0, keepdims=True)
        gains = more_gains if gains is None else gains + more_gains
        shifts = more_shifts if shifts is None else shifts + more_shifts
    sums[0:1, :] = gains
    sums[1:2, :] = shifts
    for part in range(3):
        sums[2 + part : 3 + part, 0:BLOCK] = jnp.sum(joined[part].astype(F32), axis=0, keepdims=True)


def small_kernel(ids, hidden_sums, mid_sums, input_sums, table, *outs):
    for s in range(GROUP):
        out = outs[s]
        out[...] = jnp.zeros(out.shape, F32)
        out[0:1, :] = hidden_sums[0:1, :]
        for part in range(3):
            out[1 + part : 2 + part, 0:BLOCK] = input_sums[2 + part : 3 + part, 0:BLOCK]
        out[4 : 4 + HEADS, 0:REL] = table[0:HEADS, :]
        lanes = slice(s * BLOCK, (s + 1) * BLOCK)
        out[10:11, 0:BLOCK] = hidden_sums[1:2, lanes]
        out[11:12, 0:BLOCK] = mid_sums[0:1, lanes]
        out[12:13, 0:BLOCK] = mid_sums[1:2, lanes]
        out[13:14, 0:BLOCK] = mid_sums[2:3, lanes]
        out[14:15, 0:BLOCK] = input_sums[0:1, lanes]
        out[15:16, 0:BLOCK] = input_sums[1:2, lanes]


def ordered_sum_kernel(ids, a, b, c, d, out, held):
    z = ids[1]
    for s, piece in enumerate((a, b, c, d)):
        held[(z + s) % GROUP] = piece[...]
    out[...] = ((held[0] + held[1]) + held[2]) + held[3]


def output_kernel(ids, middle, total, vectors_a, vectors_b, vectors_c, vectors_d, o0, o1, o2, o3):
    bias = wide_vector((vectors_a, vectors_b, vectors_c, vectors_d), 5)
    result = (middle[...] + total[...] + bias).astype(BF)
    for s, out in enumerate((o0, o1, o2, o3)):
        out[...] = result[:, s * BLOCK : (s + 1) * BLOCK]


def input_grad_kernel(ids, total, tokens, own_mid, va, vb, vc, vd, o0, o1, o2, o3):
    gain = wide_vector((va, vb, vc, vd), 0)
    scaled, inverse = norm_stats(tokens[...].astype(F32))
    e = total[...] * gain
    part = e - jnp.mean(e, axis=-1, keepdims=True) - scaled * jnp.mean(e * scaled, axis=-1, keepdims=True)
    result = (own_mid[...] + inverse * part).astype(BF)
    for s, out in enumerate((o0, o1, o2, o3)):
        out[...] = result[:, s * BLOCK : (s + 1) * BLOCK]


def wide_store(out, piece, begin, step, offset):
    count = piece.shape[0]
    for k in range(3):
        out[pl.ds(begin * step + offset + k, count, stride=step), :] = piece[:, k * 128 : (k + 1) * 128]


def finish_hidden_kernel(ids, mine_c, other_c, mine_e, other_e, out_c, out_e):
    x = ids[0]
    rows = HALF // 2
    wide_store(out_c, mine_c[...].astype(F32), x * rows, 3, 0)
    wide_store(out_c, other_c[...].astype(F32), (1 - x) * rows, 3, 0)
    rows = BLOCK // 2
    out_e[pl.ds(aligned(x * rows, 8), rows), :] = mine_e[...].astype(F32)
    out_e[pl.ds(aligned((1 - x) * rows, 8), rows), :] = other_e[...].astype(F32)


def finish_joined_kernel(ids, mine_q, other_q, mine_o, other_o, out_q, out_o):
    x = ids[0]
    rows = BLOCK // 4
    wide_store(out_o, mine_o[...].astype(F32), x * rows, 3, 0)
    wide_store(out_o, other_o[...].astype(F32), (1 - x) * rows, 3, 0)
    for part in range(3):
        wide_store(out_q, mine_q[part].astype(F32), x * rows, 9, part * 3)
        wide_store(out_q, other_q[part].astype(F32), (1 - x) * rows, 9, part * 3)


def local_program(dp_size, row_size, col_size):
    def turn(value, shift):
        return lax.ppermute(value, "row", [(i, (i + shift) % row_size) for i in range(row_size)])

    def flip(value, bits):
        return lax.ppermute(value, "col", [(i, i ^ bits) for i in range(col_size)])

    def swap(value, bits=1):
        return lax.ppermute(value, "dp", [(i, i ^ bits) for i in range(dp_size)])

    def add(first, second):
        return first.astype(F32) + second.astype(F32)

    def swap_rest(value):
        bits = 2
        while bits < dp_size:
            value = add(value, swap(value, bits)).astype(value.dtype)
            bits *= 2
        return value

    def gather_weight(own, half):
        mine = [turn(half, s) for s in range(1, row_size)]
        return [own] + mine + [swap(piece) for piece in mine]

    def reduce_weight(keep, send):
        came = swap(send)
        summed = [add(keep[s], came[s]).astype(BF) for s in range(row_size)]
        parts = [summed[0]] + [turn(summed[s], -s) for s in range(1, row_size)]
        total = parts[0].astype(F32)
        for piece in parts[1:]:
            total = total + piece.astype(F32)
        total = swap_rest(total.astype(BF))
        return total, swap(total)

    def spread_windows(paired, ids):
        slots = run(order_kernel, [((CELLS, BLOCK), BF)] * GROUP, [], ids, paired)
        slots = [slots[0]] + [turn(slots[s], s) for s in range(1, row_size)]
        sibling = [flip(v, 1) for v in slots]
        across = [flip(v, 2) for v in slots]
        corner = [flip(v, 1) for v in across]
        return slots + sibling + across + corner

    def local(
        inputs, cotangent, slot_mask, region_ids, offset_index, first_gain, first_shift,
        query_key_value, query_value_bias, position_table, output_weight, output_bias,
        second_gain, second_shift, expand_weight, expand_bias, contract_weight, contract_bias,
    ):
        dp = lax.axis_index("dp").astype(jnp.int32)
        row = lax.axis_index("row").astype(jnp.int32)
        col = lax.axis_index("col").astype(jnp.int32)
        x = dp % 2
        ids = jnp.stack([x, row, col, dp])

        def half_of(value, axis):
            size = value.shape[axis] // 2
            return lax.dynamic_slice_in_dim(value, x * size, size, axis)

        joined_own = query_key_value.reshape(BLOCK // 2, 3, HALF).transpose(1, 0, 2)
        out_own = output_weight.reshape(BLOCK // 2, HALF)
        contract_own = contract_weight.reshape(HALF, HALF)
        vector_own = jnp.pad(
            jnp.stack([first_gain, first_shift, output_bias, second_gain, second_shift, contract_bias]),
            ((0, 2), (0, 0)),
        )
        pieces = spread_windows(inputs.reshape(inputs.shape[0], HALF), ids)
        joined_all = gather_weight(joined_own, half_of(joined_own, 1))
        vectors = [vector_own] + [turn(vector_own, s) for s in range(1, row_size)]
        out_all = gather_weight(out_own, half_of(out_own, 0))
        expand_all = gather_weight(expand_weight, half_of(expand_weight, 0))
        cot_pieces = spread_windows(cotangent.reshape(cotangent.shape[0], HALF), ids)
        contract_all = gather_weight(contract_own, half_of(contract_own, 0))

        labels = (
            region_ids.reshape(2, WIN, 2, WIN).transpose(0, 2, 1, 3).reshape(GROUP, CELLS)
        )
        (bias,) = run(
            bias_kernel, [((HEADS, CELLS, CELLS), F32)],
            [((24, REL), F32), ((WIN, 8, 3 * 128), F32), ((CELLS, CELLS), F32)],
            ids, position_table.T, offset_index, labels, labels.T,
        )
        (joined_weight,) = run(
            qkv_weights_kernel, [((3, WIDTH, BLOCK), BF)], [((GROUP, 3, BLOCK // 2, HALF), BF)], ids, *joined_all
        )
        (out_weight,) = run(
            out_weights_kernel, [((BLOCK, WIDTH), BF)], [((GROUP, BLOCK // 2, HALF), BF)], ids, *out_all
        )
        tokens, normed_one, queries, keys, values, probs, attended = run(
            attend_kernel,
            [((TOKENS, WIDTH), BF)] * 2 + [((TOKENS, BLOCK), BF)] * 3
            + [((GROUP * HEADS, CELLS, CELLS), BF), ((2 * CELLS, HALF), BF)],
            [], ids, *pieces, *vectors, joined_weight, query_value_bias, bias,
        )
        attended_all = [attended, flip(attended, 1), flip(attended, 2)]
        attended_all.append(flip(attended_all[2], 1))
        out_square = [out_weight, flip(out_weight, 1), flip(out_weight, 2)]
        out_square.append(flip(out_square[2], 1))
        (expand_square,) = run(
            expand_weights_kernel, [((WIDTH, WIDTH), BF)], [((GROUP, BLOCK, WIDTH), BF)], ids, *expand_all
        )
        hidden_bias = expand_bias.reshape(HALF, 2).T.reshape(1, WIDTH)
        middle, normed_two, hidden, slope = run(
            expand_kernel,
            [((TOKENS, WIDTH), F32), ((TOKENS, WIDTH), BF), ((TOKENS, WIDTH), BF), ((TOKENS, WIDTH), F32)],
            [((TOKENS, WIDTH), BF), ((WIDTH, WIDTH), BF)],
            ids, tokens, *attended_all, *out_square, *vectors, expand_square, hidden_bias,
        )
        (contract_square,) = run(
            contract_weights_kernel, [((WIDTH, WIDTH), BF)], [((GROUP, HALF, HALF), BF)], ids, *contract_all
        )
        (upstream,) = run_slots(ids, slot_mask, cot_pieces)
        two = (2 * CELLS, WIDTH)
        pre_grad, keep, send = run(
            hidden_back_kernel, [((TOKENS, WIDTH), BF), (two, F32), (two, BF)], [],
            ids, upstream, contract_square, slope, expand_square,
        )
        even_half = add(keep, flip(send, 1)).astype(BF)
        came = flip(even_half, 2)
        even_total = (
            add(even_half.reshape(2, CELLS, WIDTH), came.reshape(2, CELLS, WIDTH)[::-1])
            .astype(BF)
            .reshape(2 * CELLS, WIDTH)
        )
        odd_total = flip(even_total, 1)
        keep_c, send_c, keep_e, send_e, keep_out, send_out, hidden_sums = run(
            hidden_grads_kernel,
            [((GROUP, HALF // 2, HALF), BF)] * 2 + [((GROUP, BLOCK // 2, WIDTH), BF)] * 2
            + [(two, F32), (two, BF), ((8, WIDTH), F32)],
            [((GROUP, HALF, HALF), BF), ((WIDTH, WIDTH), BF)],
            ids, upstream, hidden, normed_two, pre_grad, contract_square,
        )
        mine_c, other_c = reduce_weight(keep_c, send_c)
        mine_e, other_e = reduce_weight(keep_e, send_e)
        own_mid, mid_low, joined_grad, bias_grad, keep, send, mid_sums = run(
            attend_back_kernel,
            [((CELLS, WIDTH), F32), ((TOKENS, WIDTH), BF), ((3, TOKENS, BLOCK), BF),
             ((HEADS, CELLS, CELLS), F32), (two, F32), (two, BF), ((8, WIDTH), F32)],
            [((TOKENS, BLOCK), BF)],
            ids, even_total, odd_total, middle, upstream, *vectors, out_weight,
            queries, keys, values, probs, joined_weight,
        )
        keep_q, send_q, keep_o, send_o, input_sums = run(
            joined_grads_kernel,
            [((GROUP, 3, BLOCK // 4, HALF), BF)] * 2 + [((GROUP, BLOCK // 4, HALF), BF)] * 2 + [((8, WIDTH), F32)],
            [((3, HALF, HALF), BF), ((GROUP, BLOCK // 2, HALF), BF)],
            ids, normed_one, joined_grad, attended, mid_low, tokens, keep, send,
        )
        mine_q, other_q = reduce_weight(keep_q, send_q)
        mine_o, other_o = reduce_weight(keep_o, send_o)

        def own_window(keep, send):
            pair = add(keep, flip(send, 1))
            return add(pair[:CELLS], flip(pair[CELLS:].astype(BF), 2))

        def give_back(slots):
            return [slots[0]] + [turn(slots[s], -s) for s in range(1, row_size)]

        grad_slots = run(
            input_grad_kernel, [((CELLS, BLOCK), BF)] * GROUP, [],
            ids, own_window(keep, send), tokens[:CELLS], own_mid, *vectors,
        )
        (input_gradient,) = run(
            restore_wide_kernel, [((864, 128), F32)], [((2 * CELLS, HALF), F32)], ids, *give_back(grad_slots)
        )
        out_slots = run(
            output_kernel, [((CELLS, BLOCK), BF)] * GROUP, [],
            ids, middle[:CELLS], own_window(keep_out, send_out), *vectors,
        )
        (layer_output,) = run(restore_kernel, [((2 * CELLS, HALF), BF)], [], ids, *give_back(out_slots))

        (table_grad,) = run(
            table_kernel, [((8, REL), F32)], [((WIN, 8, 3 * 128), F32), ((WIN, 3 * 128), F32)],
            ids, bias_grad, offset_index,
        )
        small = run(
            small_kernel, [((16, WIDTH), F32)] * GROUP, [], ids, hidden_sums, mid_sums, input_sums, table_grad
        )
        (small_sum,) = run(
            ordered_sum_kernel, [((16, WIDTH), F32)], [((GROUP, 16, WIDTH), F32)], ids, *give_back(small)
        )
        small_sum = small_sum + swap(small_sum)
        small_sum = swap_rest(small_sum)
        rows = small_sum[10:16, :BLOCK]
        rows = rows + flip(rows, 1)
        rows = rows + flip(rows, 2)
        out_c, out_e = run(
            finish_hidden_kernel, [((HALF * 3, 128), F32), ((BLOCK, WIDTH), F32)], [],
            ids, mine_c, other_c, mine_e, other_e,
        )
        out_q, out_o = run(
            finish_joined_kernel, [((BLOCK // 2 * 9, 128), F32), ((BLOCK // 2 * 3, 128), F32)], [],
            ids, mine_q, other_q, mine_o, other_o,
        )
        return (
            layer_output.reshape(inputs.shape),
            input_gradient.reshape(inputs.shape),
            rows[4],
            rows[5],
            out_q.reshape(query_key_value.shape),
            jnp.stack([small_sum[1, :BLOCK], small_sum[3, :BLOCK]]),
            small_sum[4 : 4 + HEADS, :REL].T,
            out_o.reshape(output_weight.shape),
            rows[1],
            rows[2],
            rows[3],
            out_e,
            small_sum[0].reshape(2, HALF).T.reshape(WIDTH),
            out_c.reshape(contract_weight.shape),
            rows[0],
        )

    return local


def run_slots(ids, slot_mask, pieces):
    vmem = pl.BlockSpec(memory_space=pltpu.VMEM)
    smem = pl.BlockSpec(memory_space=pltpu.SMEM)
    return pl.pallas_call(
        upstream_kernel,
        out_shape=[jax.ShapeDtypeStruct((TOKENS, WIDTH), BF)],
        in_specs=[smem, smem] + [vmem] * len(pieces),
        out_specs=[vmem],
        compiler_params=pltpu.CompilerParams(vmem_limit_bytes=40 * 1024 * 1024),
        name="upstream_kernel",
    )(ids, slot_mask, *pieces)


def solution(mesh):
    in_specs = (
        P(("dp", "col"), "row", None),
        P(("dp", "col"), "row", None),
        P(),
        P(),
        P(),
        P("row"),
        P("row"),
        P("row", None, "col", None),
        P(None, "col"),
        P(None, "col"),
        P("col", "row", None),
        P("row"),
        P("row"),
        P("row"),
        P("row", "col"),
        P("col"),
        P("col", "row", None),
        P("row"),
    )
    out_specs = (
        P(("dp", "col"), "row", None),
        P(("dp", "col"), "row", None),
        P("row"),
        P("row"),
        P("row", None, "col", None),
        P(None, "col"),
        P(None, "col"),
        P("col", "row", None),
        P("row"),
        P("row"),
        P("row"),
        P("row", "col"),
        P("col"),
        P("col", "row", None),
        P("row"),
    )
    local = local_program(mesh.shape["dp"], mesh.shape["row"], mesh.shape["col"])
    return jax.shard_map(local, mesh=mesh, in_specs=in_specs, out_specs=out_specs, check_vma=False)
```

```python
import types

import jax
import jax.numpy as jnp
from jax import lax
from jax.experimental import pallas as pl
from jax.experimental.pallas import tpu as pltpu
from jax.sharding import PartitionSpec as P

HEAD_DIM = 32
SIDE = 24
WIN = 12
SHIFT = 6
REL = 529
CELLS = WIN * WIN
NORM_EPS = 1e-05
MASK_FILL = -100.0
BF = jnp.bfloat16
F32 = jnp.float32
NT = (((1,), (1,)), ((), ()))
TN = (((0,), (0,)), ((), ()))
BLOCK = 192
WIDTH = 768
HALF = 384
GROUP = 4
TOKENS = GROUP * CELLS
HEADS = BLOCK // HEAD_DIM
VMEM_MIB = 24
ORDER_MIB = 60
ROOT_HALF = 0.7071067811865476
ROOT_TWO_PI_INV = 0.3989422804014327


def dot(a, b):
    return jnp.dot(a, b, preferred_element_type=F32)


def dot_nt(a, b):
    return lax.dot_general(a, b, NT, preferred_element_type=F32)


def dot_tn(a, b):
    return lax.dot_general(a, b, TN, preferred_element_type=F32)


def iota(shape, dim):
    return lax.broadcasted_iota(jnp.int32, shape, dim)


def aligned(value, step):
    return pl.multiple_of(value, step)


MICROS = 10


def cost_of(kernel):
    micros = 0.01 if kernel in CHEAP else MICROS
    return pl.CostEstimate(flops=int(micros * 1.1e9), bytes_accessed=int(micros * 3.6e6), transcendentals=0)


def run(kernel, outs, scratch, *arrays, scalars=(), mib=VMEM_MIB, after=()):
    vmem = pl.BlockSpec(memory_space=pltpu.VMEM)
    smem = pl.BlockSpec(memory_space=pltpu.SMEM)
    anywhere = pl.BlockSpec(memory_space=pl.ANY)
    given = len(scalars) + len(arrays)
    made = given + len(after) + len(outs)

    def body(*refs):
        dp = lax.axis_index("dp")
        ids = (dp % 2, lax.axis_index("row"), lax.axis_index("col"), dp)
        kernel(ids, *refs[:given], *refs[given + len(after) : made], *refs[made + 1 :])
        refs[made][...] = jnp.zeros(refs[made].shape, F32)

    return pl.pallas_call(
        body,
        out_shape=[jax.ShapeDtypeStruct(shape, dtype) for shape, dtype in (*outs, ((8, 128), F32))],
        in_specs=[smem] * len(scalars) + [vmem] * len(arrays) + [anywhere] * len(after),
        out_specs=[vmem] * (len(outs) + 1),
        scratch_shapes=[pltpu.VMEM(shape, dtype) for shape, dtype in scratch],
        compiler_params=pltpu.CompilerParams(vmem_limit_bytes=mib * 1024 * 1024),
        cost_estimate=cost_of(kernel),
        name=kernel.__name__,
    )(*scalars, *arrays, *after)


def place(window, position):
    row = (position * 171) >> 11
    col = position - row * WIN
    row = row + (window // 2) * WIN + SHIFT
    col = col + (window % 2) * WIN + SHIFT
    row = jnp.where(row >= SIDE, row - SIDE, row)
    col = jnp.where(col >= SIDE, col - SIDE, col)
    token = row * SIDE + col
    return token >> 1, token & 1


def window_rows(paired_even, paired_odd, window, begin, rows):
    count = paired_even.shape[0]
    half, parity = place(window, iota((rows, count), 0) + begin)
    hit = half == iota((rows, count), 1)
    pick_even = jnp.where(hit & (parity == 0), 1.0, 0.0).astype(BF)
    pick_odd = jnp.where(hit & (parity == 1), 1.0, 0.0).astype(BF)
    return dot(pick_even, paired_even) + dot(pick_odd, paired_odd)


LINES = CELLS // 2
FIRST = 2 * CELLS // 2 + 16
QUARTER = BLOCK // 4
STACK = HEADS * CELLS + 32
CHUNKS = ((0, 256), (256, 256), (512, 256), (768, 128))
ATT = 2 * CELLS


def order_kernel(ids, vectors, paired, cotangent, joined, out_own, o0, o1, o2, o3, held):
    z = ids[1]
    sources = [(v[:, :BLOCK], v[:, BLOCK:]) for v in (paired, cotangent)]
    held[...] = jnp.zeros(held.shape, F32)
    whole = vectors[...]
    high = whole.astype(BF).astype(F32)
    rest = whole - high
    middle = rest.astype(BF).astype(F32)
    begin = aligned(ids[0] * QUARTER, 16)
    for s, out in enumerate((o0, o1, o2, o3)):
        held[s, 2 * LINES : 2 * LINES + 6, :BLOCK] = high
        held[s, 2 * LINES : 2 * LINES + 6, BLOCK:] = middle
        held[s, 2 * LINES + 8 : 2 * LINES + 14, :BLOCK] = rest - middle
        for n, (even, odd) in enumerate(sources):
            for k in range(2):
                held[s, n * LINES : (n + 1) * LINES, k * BLOCK : (k + 1) * BLOCK] = window_rows(
                    even, odd, (z + s) % GROUP, k * LINES, LINES
                )
        out[0:FIRST, :] = held[s].astype(BF)
        for part in range(3):
            out[FIRST + part * QUARTER : FIRST + (part + 1) * QUARTER, :] = joined[part, pl.ds(begin, QUARTER), :]
        out[FIRST + 3 * QUARTER :, :] = out_own[pl.ds(begin, QUARTER), :]


def unpack_kernel(ids, slots, a, b, c, d, tokens, vectors, stack):
    flag = slots[ids[3] * GROUP + ids[2]] != 0
    vectors[...] = jnp.zeros(vectors.shape, F32)
    for s, piece in enumerate((a, b, c, d)):
        lanes = slice(s * BLOCK, (s + 1) * BLOCK)
        whole = piece[0:FIRST, :].astype(F32)
        for n in range(2):
            part = whole[n * LINES : (n + 1) * LINES]
            part = jnp.concatenate([part[:, :BLOCK], part[:, BLOCK:]], axis=0)
            if n == 1:
                part = jnp.where(flag, part, jnp.zeros_like(part))
            tokens[n * CELLS : (n + 1) * CELLS, lanes] = part.astype(BF)
        line = 2 * LINES
        vectors[0:6, lanes] = (
            whole[line : line + 6, :BLOCK] + whole[line : line + 6, BLOCK:] + whole[line + 8 : line + 14, :BLOCK]
        )
        if s > 0:
            stack[s - 1] = piece[FIRST:, :]


def couple_kernel(ids, a, b, out):
    out[0] = a[...]
    out[1] = b[...]


def half_kernel(ids, whole, out):
    rows = out.shape[0]
    out[...] = whole[pl.ds(aligned(ids[0] * rows, 16), rows), :]


def pass_kernel(ids, whole, out):
    out[...] = whole[...]


def stack_kernel(ids, a, b, c, out):
    for s, piece in enumerate((a, b, c)):
        out[s] = piece[...]


def restore_halves(ids, pieces):
    z = ids[1]
    count = SIDE * SIDE // 2
    even = odd = None
    for s in range(GROUP):
        half, parity = place((z + s) % GROUP, iota((count, CELLS), 1))
        hit = half == iota((count, CELLS), 0)
        pick_even = jnp.where(hit & (parity == 0), 1.0, 0.0).astype(BF)
        pick_odd = jnp.where(hit & (parity == 1), 1.0, 0.0).astype(BF)
        piece = pieces[s]
        more_even = dot(pick_even, piece)
        more_odd = dot(pick_odd, piece)
        even = more_even if even is None else even + more_even
        odd = more_odd if odd is None else odd + more_odd
    return even, odd


def restore_kernel(ids, a, b, c, d, out):
    even, odd = restore_halves(ids, [window_piece(v[v.shape[0] - EXTRA :, :]) for v in (a, b, c, d)])
    out[:, :BLOCK] = even.astype(BF)
    out[:, BLOCK:] = odd.astype(BF)


def restore_wide_kernel(ids, a, b, c, d, out, whole):
    even, odd = restore_halves(ids, [window_piece(v[v.shape[0] - EXTRA :, :]) for v in (a, b, c, d)])
    whole[:, :BLOCK] = even
    whole[:, BLOCK:] = odd
    count = whole.shape[0]
    for k in range(3):
        out[pl.ds(k, count, stride=3), :] = whole[:, k * 128 : (k + 1) * 128]


def pair_picks(rows):
    low = iota((rows, rows // 2), 0)
    high = iota((rows, rows // 2), 1)
    pick_even = jnp.where(low == 2 * high, 1.0, 0.0).astype(BF)
    pick_odd = jnp.where(low == 2 * high + 1, 1.0, 0.0).astype(BF)
    return pick_even, pick_odd


def hidden_perm():
    natural = iota((WIDTH, WIDTH), 0)
    split = iota((WIDTH, WIDTH), 1)
    wanted = jnp.where(split < HALF, 2 * split, 2 * split - (WIDTH - 1))
    return jnp.where(natural == wanted, 1.0, 0.0).astype(BF)


def put_halves(ids, held, s, where, rows, mine, other):
    x = ids[0]
    held[(s, *where, pl.ds(aligned(x * rows, 16), rows), slice(None))] = mine
    held[(s, *where, pl.ds(aligned((1 - x) * rows, 16), rows), slice(None))] = other


def first_weights_kernel(ids, own, own_out, mine, other, out, out_square, held):
    pick_even, pick_odd = pair_picks(BLOCK)
    for part in range(4):
        held[0, part] = own[part] if part < 3 else own_out[...]
        lines = slice(part * QUARTER, (part + 1) * QUARTER)
        for s in range(1, GROUP):
            put_halves(ids, held, s, (part,), QUARTER, mine[s - 1, lines, :], other[s - 1, lines, :])
    for s in range(GROUP):
        for part in range(4):
            block = (dot(pick_even, held[s, part, :, :BLOCK]) + dot(pick_odd, held[s, part, :, BLOCK:])).astype(BF)
            if part < 3:
                out[part, s * BLOCK : (s + 1) * BLOCK, :] = block
            else:
                out_square[:, s * BLOCK : (s + 1) * BLOCK] = block


def expand_weights_kernel(ids, own, mine, other, bias, out, out_bias, held, rows):
    perm = hidden_perm()
    held[0] = own[...]
    for s in range(1, GROUP):
        put_halves(ids, held, s, (), BLOCK // 2, mine[s - 1], other[s - 1])
    for s in range(GROUP):
        out[s * BLOCK : (s + 1) * BLOCK, :] = dot(held[s], perm).astype(BF)
    high = bias[...].astype(BF).astype(F32)
    rest = bias[...] - high
    middle = rest.astype(BF).astype(F32)
    rows[...] = jnp.zeros(rows.shape, F32)
    rows[0:1, :] = high
    rows[1:2, :] = middle
    rows[2:3, :] = rest - middle
    found = dot(rows[...].astype(BF), perm)
    out_bias[...] = found[0:1] + found[1:2] + found[2:3]


def contract_weights_kernel(ids, own, m1, m2, m3, out):
    for s, piece in enumerate((own, m1, m2, m3)):
        for q in range(2):
            out[q * HALF : (q + 1) * HALF, s * BLOCK : (s + 1) * BLOCK] = piece[:, q * BLOCK : (q + 1) * BLOCK]


def entry_hits(offset, index):
    row = offset[pl.ds(index, 1), :]
    return jnp.where(iota((REL, CELLS), 0) == row, 1.0, 0.0).astype(BF)


STRIP = 3 * 128
FAR = WIN - 1
SPAN = FAR * WIN


def lane_col():
    lane = iota((8, STRIP), 1)
    return lane - ((lane * 171) >> 11) * WIN


def bias_kernel(ids, table, offset, labels, labels_t, out, parts, strips, mask):
    z = ids[1]
    parts[...] = jnp.zeros(parts.shape, F32)
    whole = table[...]
    high = whole.astype(BF).astype(F32)
    rest = whole - high
    middle = rest.astype(BF).astype(F32)
    parts[0:HEADS, :] = high
    parts[8 : 8 + HEADS, :] = middle
    parts[16 : 16 + HEADS, :] = rest - middle
    split = parts[...].astype(BF)
    row_label = labels[pl.ds(z, 1), :]
    col_label = jnp.sum(jnp.where(iota((CELLS, GROUP), 1) == z, labels_t[...], 0), axis=1, keepdims=True)
    mask[...] = jnp.where(row_label == col_label, 0.0, MASK_FILL)
    sides = []
    for c in (FAR, 0):
        rows = []
        for r in (FAR, 0):
            found = dot(split, entry_hits(offset, r * WIN + c))
            rows.append((found[0:8] + found[8:16]) + found[16:24])
        sides.append(
            jnp.concatenate([rows[0], rows[1][:, WIN:], jnp.zeros((8, STRIP - CELLS - SPAN), F32)], axis=1)
        )
    col = lane_col()
    for c in range(WIN):
        near = pltpu.roll(sides[0], (STRIP - (FAR - c)) % STRIP, 1)
        far = pltpu.roll(sides[1], c, 1)
        strips[c] = jnp.where(col <= c, near, far)
    for h in range(HEADS):
        strip = strips[:, h, :]
        for r in range(WIN):
            begin = (FAR - r) * WIN
            out[r * WIN : (r + 1) * WIN, h * CELLS : (h + 1) * CELLS] = (
                strip[:, begin : begin + CELLS] + mask[r * WIN : (r + 1) * WIN, :]
            )
    out[:, HEADS * CELLS :] = jnp.zeros((CELLS, STACK - HEADS * CELLS), F32)


def table_sums(grads, offset, strips, wide):
    for h in range(HEADS):
        wide[h] = jnp.zeros(wide.shape[1:], F32)
        for r in range(WIN):
            begin = (FAR - r) * WIN
            wide[h, :, begin : begin + CELLS] += grads[r * WIN : (r + 1) * WIN, h * CELLS : (h + 1) * CELLS]
        strips[:, h, :] = wide[h]
    col = lane_col()
    zero = jnp.zeros((8, STRIP), F32)
    near = far = zero
    for c in range(WIN):
        strip = strips[c]
        near = near + pltpu.roll(jnp.where(col <= c, strip, zero), FAR - c, 1)
        far = far + pltpu.roll(jnp.where(col <= c, zero, strip), (STRIP - c) % STRIP, 1)
    total = None
    for c, side in ((FAR, near), (0, far)):
        upper = side[:, 0:CELLS]
        lower = jnp.concatenate([jnp.zeros((8, WIN), F32), side[:, CELLS : CELLS + SPAN]], axis=1)
        for r, piece in ((FAR, upper), (0, lower)):
            high = piece.astype(BF).astype(F32)
            both = jnp.concatenate([high, piece - high], axis=0).astype(BF)
            found = dot_nt(both, entry_hits(offset, r * WIN + c))
            total = found if total is None else total + found
    return total[0:8] + total[8:16]


def norm_stats(values):
    centre = jnp.mean(values, axis=-1, keepdims=True)
    moved = values - centre
    inverse = lax.rsqrt(jnp.mean(moved * moved, axis=-1, keepdims=True) + NORM_EPS)
    return moved * inverse, inverse


def turned(block):
    return block.astype(F32).T.astype(BF)


def stack_heads(block, lane_head, out):
    for h in range(HEADS):
        out[h * CELLS : (h + 1) * CELLS, :] = jnp.where(lane_head == h, block, jnp.zeros_like(block))
    out[HEADS * CELLS :, :] = jnp.zeros((STACK - HEADS * CELLS, BLOCK), BF)


def pick_heads(wide, held):
    for h in range(HEADS):
        lines = slice(h * HEAD_DIM, (h + 1) * HEAD_DIM)
        held[lines, :] = wide[lines, h * CELLS : (h + 1) * CELLS]
    return held[...].T


def attend_kernel(ids, *refs):
    pieces = refs[0:2]
    vectors, weights, head_bias, bias, out_weight = refs[2:7]
    tokens, normed, queries, keys, values, probs, attended = refs[7:14]
    stacked, held = refs[14:16]
    gain = vectors[0:1, :]
    shift = vectors[1:2, :]
    for j in range(GROUP):
        tokens[j * CELLS : (j + 1) * CELLS, :] = pieces[j & 1][j >> 1, 0:CELLS, :]

    @pl.loop(0, GROUP)
    def _(w):
        rows = pl.ds(aligned(w * CELLS, 16), CELLS)
        scaled, _ = norm_stats(tokens[rows, :].astype(F32))
        normed[rows, :] = (scaled * gain + shift).astype(BF)

    scale = float(HEAD_DIM) ** (-0.5)
    whole = normed[...]
    queries[...] = ((dot(whole, weights[0]) + head_bias[0:1, :]) * scale).astype(BF)
    keys[...] = dot(whole, weights[1]).astype(BF)
    values[...] = (dot(whole, weights[2]) + head_bias[1:2, :]).astype(BF)
    lane_head = iota((CELLS, BLOCK), 1) // HEAD_DIM
    for w in range(GROUP):
        rows = pl.ds(w * CELLS, CELLS)
        key = keys[rows, :]
        stack_heads(queries[rows, :], lane_head, stacked.at[w])
        for begin, count in CHUNKS:
            scores = dot_nt(key, stacked[w, begin : begin + count, :]) + bias[:, begin : begin + count]
            powers = jnp.exp(scores - jnp.max(scores, axis=0, keepdims=True))
            share = powers * (1.0 / jnp.sum(powers, axis=0, keepdims=True))
            probs[w, :, begin : begin + count] = share.astype(BF)
        total = pick_heads(dot(turned(values[rows, :]), probs[w]), held.at[w])
        attended[(w & 1) * CELLS : (w & 1) * CELLS + CELLS, (w >> 1) * BLOCK : (w >> 1) * BLOCK + BLOCK] = (
            total.astype(BF)
        )
    for k in range(2):
        attended[ATT + k * BLOCK : ATT + (k + 1) * BLOCK, :] = out_weight[:, k * HALF : (k + 1) * HALF]


def expand_kernel(ids, *refs):
    tokens = refs[0]
    attended = refs[1:3]
    vectors, weights, hidden_bias = refs[3:6]
    middle, normed, hidden, slope = refs[6:10]
    joined, square = refs[10:12]
    for j in range(GROUP):
        source = attended[j & 1]
        for k in range(2):
            square[j * BLOCK : (j + 1) * BLOCK, k * HALF : (k + 1) * HALF] = source[
                j >> 1, ATT + k * BLOCK : ATT + (k + 1) * BLOCK, :
            ]
        for i in range(GROUP):
            k = i ^ j
            joined[i * CELLS : (i + 1) * CELLS, j * BLOCK : (j + 1) * BLOCK] = source[
                j >> 1, (k & 1) * CELLS : (k & 1) * CELLS + CELLS, (k >> 1) * BLOCK : (k >> 1) * BLOCK + BLOCK
            ]
    out_bias = vectors[2:3, :]
    gain = vectors[3:4, :]
    shift = vectors[4:5, :]

    @pl.loop(0, 2)
    def _(t):
        rows = pl.ds(aligned(t * (TOKENS // 2), 16), TOKENS // 2)
        mid = tokens[rows, :].astype(F32) + dot(joined[rows, :], square[...]) + out_bias
        middle[rows, :] = mid
        scaled, _ = norm_stats(mid)
        second = (scaled * gain + shift).astype(BF)
        normed[rows, :] = second
        pre = dot(second, weights[...]) + hidden_bias[...]
        bell = 0.5 * (1.0 + lax.erf(pre * ROOT_HALF))
        hidden[rows, :] = (pre * bell).astype(BF)
        slope[rows, :] = bell + pre * (ROOT_TWO_PI_INV * jnp.exp(-0.5 * pre * pre))


def split_slots(product, keep, send):
    keep[0:CELLS, :] = product[0:CELLS].astype(keep.dtype)
    keep[CELLS:, :] = product[2 * CELLS : 3 * CELLS].astype(keep.dtype)
    send[0:CELLS, :] = product[CELLS : 2 * CELLS].astype(send.dtype)
    send[CELLS:, :] = product[3 * CELLS :].astype(send.dtype)


def hidden_back_kernel(ids, u0, u1, contract, slope, expand, upstream, pre_grad, keep, send):
    for j in range(GROUP):
        upstream[j * CELLS : (j + 1) * CELLS, :] = (u0, u1)[j & 1][j >> 1, CELLS:, :]
    pre_grad[...] = (dot_nt(upstream[...], contract[...]) * slope[...]).astype(BF)
    split_slots(dot_nt(pre_grad[...], expand[...]), keep, send)


def contract_grads_kernel(ids, u0, u1, hidden, o0, o1, o2, o3, upstream):
    for j in range(GROUP):
        upstream[j * CELLS : (j + 1) * CELLS, :] = (u0, u1)[j & 1][j >> 1, CELLS:, :]
    up = upstream[...]
    for q in range(2):
        block = dot_tn(hidden[:, q * HALF : (q + 1) * HALF], up).astype(BF)
        for s, out in enumerate((o0, o1, o2, o3)):
            out[:, q * BLOCK : (q + 1) * BLOCK] = block[:, s * BLOCK : (s + 1) * BLOCK]


def expand_grads_kernel(
    ids, upstream, hidden, normed, pre_grad, contract, keep, send, keep_out, send_out, sums, whole_e,
):
    x = ids[0]
    mixed = dot_tn(normed[...], pre_grad[...]).astype(BF)
    whole_e[...] = dot_nt(mixed, hidden_perm()).astype(BF)
    lines = BLOCK // 2
    for s in range(GROUP):
        for out, side in ((keep, x), (send, 1 - x)):
            out[s] = whole_e[pl.ds(aligned(s * BLOCK + side * lines, 16), lines), :]
    split_slots(dot(hidden[...], contract[...]), keep_out, send_out)
    sums[...] = jnp.zeros(sums.shape, F32)
    sums[0:1, :] = jnp.sum(pre_grad[...].astype(F32), axis=0, keepdims=True)
    sums[1:2, :] = jnp.sum(upstream[0:CELLS, :].astype(F32), axis=0, keepdims=True)


def attend_back_kernel(ids, *refs):
    even_total, odd_total, middle, upstream = refs[0:4]
    vectors, out_weights, queries, keys, values, probs, weights = refs[4:11]
    own_mid, mid_low, joined, bias_grad, keep, send, sums = refs[11:18]
    attended_grad, stacked, stacked_grad, scores, held = refs[18:23]
    gain = vectors[3:4, :]
    sums[...] = jnp.zeros(sums.shape, F32)
    for w in range(GROUP):
        rows = pl.ds(w * CELLS, CELLS)
        source = (even_total, odd_total)[w & 1]
        grad = source[(w >> 1) * CELLS : (w >> 1) * CELLS + CELLS, :].astype(F32)
        scaled, inverse = norm_stats(middle[rows, :])
        e = grad * gain
        part = e - jnp.mean(e, axis=-1, keepdims=True) - scaled * jnp.mean(e * scaled, axis=-1, keepdims=True)
        mid = upstream[rows, :].astype(F32) + inverse * part
        low = mid.astype(BF)
        mid_low[rows, :] = low
        if w == 0:
            own_mid[...] = mid
            sums[0:1, :] = jnp.sum(low.astype(F32), axis=0, keepdims=True)
            sums[1:2, :] = jnp.sum(grad * scaled, axis=0, keepdims=True)
            sums[2:3, :] = jnp.sum(grad, axis=0, keepdims=True)
    attended_grad[...] = dot_nt(mid_low[...], out_weights[...]).astype(BF)
    lane_head = iota((CELLS, BLOCK), 1) // HEAD_DIM
    scale = float(HEAD_DIM) ** (-0.5)
    for w in range(GROUP):
        rows = pl.ds(w * CELLS, CELLS)
        key = keys[rows, :]
        value = values[rows, :]
        stack_heads(queries[rows, :], lane_head, stacked.at[w])
        stack_heads(attended_grad[rows, :], lane_head, stacked_grad.at[w])
        for begin, count in CHUNKS:
            lanes = slice(begin, begin + count)
            share = probs[w, :, lanes].astype(F32)
            product = share * dot_nt(value, stacked_grad[w, lanes, :])
            score = (product - share * jnp.sum(product, axis=0, keepdims=True)).astype(BF)
            scores[w, :, lanes] = score
            if w == 0:
                bias_grad[:, lanes] = score.astype(F32)
            else:
                bias_grad[:, lanes] += score.astype(F32)
        value_grad = dot(probs[w], stacked_grad[w])
        key_grad = dot(scores[w], stacked[w])
        query_grad = pick_heads(dot(turned(key), scores[w]), held.at[w])
        joined[0, rows, :] = (query_grad * scale).astype(BF)
        joined[1, rows, :] = key_grad.astype(BF)
        joined[2, rows, :] = value_grad.astype(BF)
    product = dot_nt(joined[0], weights[0]) + dot_nt(joined[1], weights[1]) + dot_nt(joined[2], weights[2])
    split_slots(product, keep, send)


SMALL = 16


def joined_grads_kernel(
    ids, normed, joined, attended, mid_low, tokens, keep_in, send_in, hidden_sums, mid_sums,
    bias_grad, offset, keep, send, row_sums, whole_q, whole_o, small, small_low, strips, strip_sums,
):
    x = ids[0]
    whole = normed[...]
    picks = pair_picks(BLOCK)
    for part in range(3):
        natural = dot_tn(whole, joined[part]).astype(BF)
        for s in range(GROUP):
            for q in range(2):
                whole_q[part, s * (BLOCK // 2) : (s + 1) * (BLOCK // 2), q * BLOCK : (q + 1) * BLOCK] = dot_tn(
                    picks[q], natural[s * BLOCK : (s + 1) * BLOCK]
                ).astype(BF)
    low = mid_low[...]
    total = None
    for k in range(2):
        left = attended[0:ATT, k * BLOCK : (k + 1) * BLOCK]
        product = dot_tn(left, low[2 * k * CELLS : (2 * k + 2) * CELLS])
        total = product if total is None else total + product
    wide = total.astype(BF)
    for q in range(2):
        lines = dot_tn(picks[q], wide).astype(BF)
        for s in range(GROUP):
            whole_o[s, :, q * BLOCK : (q + 1) * BLOCK] = lines[:, s * BLOCK : (s + 1) * BLOCK]
    gains = shifts = None
    for w in range(GROUP):
        source = (keep_in, send_in)[w & 1]
        grad = source[(w >> 1) * CELLS : (w >> 1) * CELLS + CELLS, :].astype(F32)
        scaled, _ = norm_stats(tokens[w * CELLS : (w + 1) * CELLS, :].astype(F32))
        more_gains = jnp.sum(grad * scaled, axis=0, keepdims=True)
        more_shifts = jnp.sum(grad, axis=0, keepdims=True)
        gains = more_gains if gains is None else gains + more_gains
        shifts = more_shifts if shifts is None else shifts + more_shifts
    small[...] = jnp.zeros(small.shape, F32)
    table = table_sums(bias_grad, offset, strips, strip_sums)
    for s in range(GROUP):
        small[s, 0:1, :] = hidden_sums[0:1, :HALF]
        small[s, 1:2, :] = hidden_sums[0:1, HALF:]
        for part in range(3):
            small[s, 2 + part : 3 + part, 0:BLOCK] = jnp.sum(joined[part].astype(F32), axis=0, keepdims=True)
        small[s, 5 : 5 + HEADS, :] = table[0:HEADS, 0:HALF]
        small[s, 11 : 11 + HEADS, 0 : REL - HALF] = table[0:HEADS, HALF:REL]
    row_sums[...] = jnp.zeros(row_sums.shape, F32)
    row_sums[0:1, :] = hidden_sums[1:2, :]
    row_sums[1:4, :] = mid_sums[0:3, :]
    row_sums[4:5, :] = gains
    row_sums[5:6, :] = shifts
    small_low[...] = small[...].astype(BF)
    rows = BLOCK // 4
    for s in range(GROUP):
        begin = s * (BLOCK // 2)
        for out, side in ((keep, x), (send, 1 - x)):
            for part in range(3):
                out[s, part * rows : (part + 1) * rows, :] = whole_q[part, pl.ds(aligned(begin + side * rows, 16), rows), :]
            out[s, 3 * rows : 4 * rows, :] = whole_o[s, pl.ds(aligned(side * rows, 16), rows), :]
            out[s, 4 * rows :, :] = small_low[s, pl.ds(aligned(side * SMALL, 16), SMALL), :]


EXTRA = 80


def window_lines(result, s, held):
    lanes = slice(s * BLOCK, (s + 1) * BLOCK)
    held[s, 0:LINES, :BLOCK] = result[0:LINES, lanes]
    held[s, 0:LINES, BLOCK:] = result[LINES:, lanes]
    held[s, LINES:, :] = jnp.zeros((EXTRA - LINES, HALF), F32)


def window_piece(lines):
    whole = lines.astype(F32)
    return jnp.concatenate([whole[0:LINES, :BLOCK], whole[0:LINES, BLOCK:]], axis=0).astype(BF)


def expand_pack_kernel(ids, keep, came, middle, pair, came_out, vectors, o0, o1, o2, o3, held):
    total = pair[0:CELLS, :].astype(F32) + came_out[...].astype(F32)
    result = middle[0:CELLS, :] + total + vectors[5:6, :]
    lines = BLOCK // 2
    for s, out in enumerate((o0, o1, o2, o3)):
        both = keep[s].astype(F32) + came[s].astype(F32)
        out[0:lines, :] = both[:, :HALF].astype(BF)
        out[lines : 2 * lines, :] = both[:, HALF:].astype(BF)
        window_lines(result, s, held)
        out[2 * lines :, :] = held[s].astype(BF)


def row_sum_kernel(ids, mine, other, out):
    out[...] = mine[...] + other[...]


def joined_pack_kernel(ids, keep, came, pair, came_in, tokens, own_mid, vectors, row_sums, row_came, o0, o1, o2, o3, held):
    total = pair[0:CELLS, :].astype(F32) + came_in[...].astype(F32)
    scaled, inverse = norm_stats(tokens[0:CELLS, :].astype(F32))
    e = total * vectors[0:1, :]
    part = e - jnp.mean(e, axis=-1, keepdims=True) - scaled * jnp.mean(e * scaled, axis=-1, keepdims=True)
    result = own_mid[...] + inverse * part
    totals = row_sums[...] + row_came[...]
    rows = keep.shape[1]
    for s, out in enumerate((o0, o1, o2, o3)):
        out[0:rows, :] = (keep[s].astype(F32) + came[s].astype(F32)).astype(BF)
        window_lines(result, s, held)
        held[s, LINES:, :BLOCK] = totals[:, s * BLOCK : (s + 1) * BLOCK]
        out[rows:, :] = held[s].astype(BF)


def ordered_sum(ids, pieces, rows, held):
    z = ids[1]
    for s, piece in enumerate(pieces):
        held[(z + s) % GROUP] = piece[0:rows, :]
    return (
        ((held[0].astype(F32) + held[1].astype(F32)) + held[2].astype(F32)) + held[3].astype(F32)
    ).astype(BF)


def ordered_sum_kernel(ids, a, b, c, d, out, held):
    out[...] = ordered_sum(ids, (a, b, c, d), out.shape[0], held)


def joined_sum_kernel(ids, a, b, c, d, out, held, lines):
    rows = held.shape[1]
    pieces = (a, b, c, d)
    out[0:rows, :] = ordered_sum(ids, pieces, rows, held)
    for s, piece in enumerate(pieces):
        lines[(ids[1] + s) % GROUP] = piece[rows + EXTRA - 16 :, :].astype(F32)
    out[rows:, :] = (((lines[0] + lines[1]) + lines[2]) + lines[3]).astype(BF)


def expand_sum_kernel(ids, mine_c, a, b, c, d, out, held):
    out[0:HALF, :] = mine_c[...]
    out[HALF:, :] = ordered_sum(ids, (a, b, c, d), BLOCK, held)


def half_sum_kernel(ids, keep, came, out):
    out[...] = (keep[...] + came[...].astype(F32)).astype(BF)


def cross_sum_kernel(ids, kept, came, out):
    for k in range(2):
        mine = slice(k * CELLS, (k + 1) * CELLS)
        theirs = slice((1 - k) * CELLS, (2 - k) * CELLS)
        out[mine, :] = (kept[mine, :].astype(F32) + came[theirs, :].astype(F32)).astype(BF)


def wide_store(out, piece, begin, step, offset):
    count = piece.shape[0]
    for k in range(3):
        out[pl.ds(begin * step + offset + k, count, stride=step), :] = piece[:, k * 128 : (k + 1) * 128]


def finish_hidden_kernel(ids, mine, other, out_c, out_e):
    x = ids[0]
    wide_store(out_c, mine[0:HALF, :].astype(F32) + other[0:HALF, :].astype(F32), 0, 3, 0)
    lines = BLOCK // 2
    for piece, side in ((mine, x), (other, 1 - x)):
        for k in range(2):
            out_e[pl.ds(aligned(side * lines, 8), lines), k * HALF : (k + 1) * HALF] = piece[
                HALF + k * lines : HALF + (k + 1) * lines, :
            ].astype(F32)


def finish_joined_kernel(ids, mine, other, out_q, out_o, out_hidden, out_heads, out_table, r0, r1, r2, r3, r4, r5, small, line):
    x = ids[0]
    for piece, side in ((mine, x), (other, 1 - x)):
        for part in range(3):
            wide_store(out_q, piece[part * QUARTER : (part + 1) * QUARTER, :].astype(F32), side * QUARTER, 9, part * 3)
        wide_store(out_o, piece[3 * QUARTER : 4 * QUARTER, :].astype(F32), side * QUARTER, 3, 0)
        small[pl.ds(aligned(side * SMALL, 8), SMALL), :] = piece[4 * QUARTER : 4 * QUARTER + SMALL, :].astype(F32)
    line[...] = jnp.zeros(line.shape, F32)
    line[0:1, :HALF] = small[0:1, :]
    line[0:1, HALF:] = small[1:2, :]
    out_hidden[...] = dot_nt(line[...].astype(BF), hidden_perm())[0:1]
    out_heads[0:1, :] = small[2:3, :BLOCK]
    out_heads[1:2, :] = small[4:5, :BLOCK]
    out_table[:, :HALF] = small[5 : 5 + HEADS, :]
    out_table[:, HALF:] = small[11 : 11 + HEADS, 0 : REL - HALF]
    ends = []
    for piece in (mine, other):
        ends.append(piece[4 * QUARTER + SMALL :, :BLOCK].astype(F32)[8:16])
    total = ends[0] + ends[1]
    for n, out in enumerate((r0, r1, r2, r3, r4, r5)):
        out[...] = total[n : n + 1]


CHEAP = (attend_kernel, expand_weights_kernel, ordered_sum_kernel, expand_pack_kernel)


def local_program(dp_size, row_size, col_size):
    def turn(value, shift):
        return lax.ppermute(value, "row", [(i, (i + shift) % row_size) for i in range(row_size)])

    def flip(value, bits):
        return lax.ppermute(value, "col", [(i, i ^ bits) for i in range(col_size)])

    def swap(value, bits=1):
        return lax.ppermute(value, "dp", [(i, i ^ bits) for i in range(dp_size)])

    def swap_rest(value):
        bits = 2
        while bits < dp_size:
            value = (value.astype(F32) + swap(value, bits).astype(F32)).astype(value.dtype)
            bits *= 2
        return value

    def turn_all(value):
        return [turn(value, s) for s in range(1, row_size)]

    def give_back(slots):
        return [slots[0]] + [turn(slots[s], -s) for s in range(1, row_size)]

    def local(
        inputs, cotangent, slot_mask, region_ids, offset_index, first_gain, first_shift,
        query_key_value, query_value_bias, position_table, output_weight, output_bias,
        second_gain, second_shift, expand_weight, expand_bias, contract_weight, contract_bias,
    ):
        joined_own = query_key_value.reshape(BLOCK // 2, 3, HALF).transpose(1, 0, 2)
        out_own = output_weight.reshape(BLOCK // 2, HALF)
        contract_own = contract_weight.reshape(HALF, HALF)
        vector_own = jnp.stack([first_gain, first_shift, output_bias, second_gain, second_shift, contract_bias])
        last = []

        def step(kernel, outs, scratch, *arrays, **given):
            results = run(kernel, outs, scratch, *arrays, after=tuple(last), **given)
            last[:] = [results[-1]]
            return results[:-1]

        v = types.SimpleNamespace()
        two = (2 * CELLS, WIDTH)
        wide = (TOKENS, WIDTH)
        rows_j = BLOCK + SMALL

        def stage_order():
            slots = step(
                order_kernel, [((FIRST + BLOCK, HALF), BF)] * GROUP, [((GROUP, FIRST, HALF), F32)],
                vector_own, inputs.reshape(2 * CELLS, HALF), cotangent.reshape(2 * CELLS, HALF),
                joined_own, out_own, mib=ORDER_MIB,
            )
            v.slots = [slots[0]] + [turn(slots[s], s) for s in range(1, row_size)]

        def stage_bias():
            labels = region_ids.reshape(2, WIN, 2, WIN).transpose(0, 2, 1, 3).reshape(GROUP, CELLS)
            (v.bias,) = step(
                bias_kernel, [((CELLS, STACK), F32)],
                [((24, REL), F32), ((WIN, 8, STRIP), F32), ((CELLS, CELLS), F32)],
                position_table.T, offset_index.T, labels, labels.T,
            )

        def stage_unpack():
            v.own, v.vectors, v.first = step(
                unpack_kernel, [(two, BF), ((8, WIDTH), F32), ((3, BLOCK, HALF), BF)], [],
                *v.slots, scalars=(slot_mask,),
            )
            v.first_other = swap(v.first)
            v.across = flip(v.own, 2)

        def stage_half():
            (half,) = step(half_kernel, [((BLOCK // 2, WIDTH), BF)], [], expand_weight)
            v.expand_mine = turn_all(half)

        def stage_stack():
            (v.expand,) = step(stack_kernel, [((3, BLOCK // 2, WIDTH), BF)], [], *v.expand_mine)
            v.expand_other = swap(v.expand)

        def stage_couple():
            (both,) = step(couple_kernel, [((2, *two), BF)], [], v.own, v.across)
            v.tokens = (both, flip(both, 1))

        def stage_first():
            v.joined_w, v.out_w = step(
                first_weights_kernel, [((3, WIDTH, BLOCK), BF), ((BLOCK, WIDTH), BF)],
                [((GROUP, 4, BLOCK // 2, HALF), BF)], joined_own, out_own, v.first, v.first_other,
            )

        def stage_pass():
            (passed,) = step(pass_kernel, [((HALF, HALF), BF)], [], contract_own)
            v.contract = turn_all(passed)

        def stage_attend():
            v.x, v.n1, v.q, v.k, v.v, v.p, v.att = step(
                attend_kernel,
                [(wide, BF)] * 2 + [((TOKENS, BLOCK), BF)] * 3
                + [((GROUP, CELLS, STACK), BF), ((ATT + HALF, HALF), BF)],
                [((GROUP, STACK, BLOCK), BF), ((GROUP, BLOCK, CELLS), F32)], *v.tokens, v.vectors, v.joined_w, query_value_bias, v.bias, v.out_w,
            )
            v.att_across = flip(v.att, 2)

        def stage_expand_w():
            v.expand_w, v.hidden_bias = step(
                expand_weights_kernel, [((WIDTH, WIDTH), BF), ((1, WIDTH), F32)],
                [((GROUP, BLOCK, WIDTH), BF), ((8, WIDTH), F32)],
                expand_weight, v.expand, v.expand_other, expand_bias.reshape(1, WIDTH),
            )

        def stage_couple_att():
            (both,) = step(couple_kernel, [((2, ATT + HALF, HALF), BF)], [], v.att, v.att_across)
            v.attended = (both, flip(both, 1))

        def stage_expand():
            v.middle, v.n2, v.hidden, v.slope = step(
                expand_kernel, [(wide, F32), (wide, BF), (wide, BF), (wide, F32)],
                [(wide, BF), ((WIDTH, WIDTH), BF)],
                v.x, *v.attended, v.vectors, v.expand_w, v.hidden_bias,
            )

        def stage_contract_g():
            parts = step(
                contract_grads_kernel, [((HALF, HALF), BF)] * GROUP, [(wide, BF)], *v.tokens, v.hidden
            )
            v.parts_c = give_back(parts)

        def stage_contract_w():
            (v.contract_w,) = step(
                contract_weights_kernel, [((WIDTH, WIDTH), BF)], [], contract_own, *v.contract
            )

        def stage_hidden():
            v.up, v.pre, v.keep_n, send = step(
                hidden_back_kernel, [(wide, BF)] * 2 + [(two, F32), (two, BF)], [],
                *v.tokens, v.contract_w, v.slope, v.expand_w,
            )
            v.came_n = flip(send, 1)

        def stage_half_sum():
            (v.even,) = step(half_sum_kernel, [(two, BF)], [], v.keep_n, v.came_n)
            v.even_came = flip(v.even, 2)

        def stage_expand_g():
            v.keep_e, send_e, v.keep_out, send_out, v.hidden_sums = step(
                expand_grads_kernel,
                [((GROUP, BLOCK // 2, WIDTH), BF)] * 2 + [(two, F32), (two, BF), ((8, WIDTH), F32)],
                [((WIDTH, WIDTH), BF)],
                v.up, v.hidden, v.n2, v.pre, v.contract_w,
            )
            v.came_e = swap(send_e)
            v.came_out = flip(send_out, 1)

        def stage_cross():
            (v.even_total,) = step(cross_sum_kernel, [(two, BF)], [], v.even, v.even_came)
            v.odd_total = flip(v.even_total, 1)

        def stage_out_sum():
            (v.pair_out,) = step(half_sum_kernel, [(two, BF)], [], v.keep_out, v.came_out)
            v.far_out = flip(v.pair_out[CELLS:], 2)

        def stage_attend_b():
            v.own_mid, v.mid_low, v.joined_g, v.bias_g, v.keep_i, send, v.mid_sums = step(
                attend_back_kernel,
                [((CELLS, WIDTH), F32), (wide, BF), ((3, TOKENS, BLOCK), BF),
                 ((CELLS, STACK), F32), (two, F32), (two, BF), ((8, WIDTH), F32)],
                [((TOKENS, BLOCK), BF), ((GROUP, STACK, BLOCK), BF), ((GROUP, STACK, BLOCK), BF),
                 ((GROUP, CELLS, STACK), BF), ((GROUP, BLOCK, CELLS), F32)],
                v.even_total, v.odd_total, v.middle, v.up, v.vectors, v.out_w,
                v.q, v.k, v.v, v.p, v.joined_w,
            )
            v.send_i = send
            v.came_i = flip(send, 1)

        def stage_contract_s():
            (v.mine_c,) = step(
                ordered_sum_kernel, [((HALF, HALF), BF)], [((GROUP, HALF, HALF), BF)], *v.parts_c
            )

        def stage_expand_p():
            parts = step(
                expand_pack_kernel, [((BLOCK + EXTRA, HALF), BF)] * GROUP, [((GROUP, EXTRA, HALF), F32)],
                v.keep_e, v.came_e, v.middle, v.pair_out, v.far_out, v.vectors,
            )
            v.parts_e = give_back(parts)

        def stage_in_sum():
            (v.pair_in,) = step(half_sum_kernel, [(two, BF)], [], v.keep_i, v.came_i)
            v.far_in = flip(v.pair_in[CELLS:], 2)

        def stage_joined():
            v.keep_j, send, v.row_sums = step(
                joined_grads_kernel, [((GROUP, rows_j, HALF), BF)] * 2 + [((8, WIDTH), F32)],
                [((3, HALF, HALF), BF), ((GROUP, BLOCK // 2, HALF), BF),
                 ((GROUP, 2 * SMALL, HALF), F32), ((GROUP, 2 * SMALL, HALF), BF),
                 ((WIN, 8, STRIP), F32), ((HEADS, WIN, STRIP), F32)],
                v.n1, v.joined_g, v.att, v.mid_low, v.x, v.keep_i, v.send_i,
                v.hidden_sums, v.mid_sums, v.bias_g, offset_index.T,
            )
            v.came_j = swap(send)
            v.row_came = flip(v.row_sums, 1)

        def stage_rows():
            (v.row_pair,) = step(row_sum_kernel, [((8, WIDTH), F32)], [], v.row_sums, v.row_came)
            v.row_far = flip(v.row_pair, 2)

        def stage_expand_s():
            (mine,) = step(
                expand_sum_kernel, [((HALF + BLOCK, HALF), BF)], [((GROUP, BLOCK, HALF), BF)],
                v.mine_c, *v.parts_e,
            )
            v.mine_h = swap_rest(mine)
            v.other_h = swap(v.mine_h)

        def stage_joined_p():
            parts = step(
                joined_pack_kernel, [((rows_j + EXTRA, HALF), BF)] * GROUP, [((GROUP, EXTRA, HALF), F32)],
                v.keep_j, v.came_j, v.pair_in, v.far_in, v.x, v.own_mid, v.vectors,
                v.row_pair, v.row_far,
            )
            v.parts_j = give_back(parts)

        def stage_restore():
            (v.layer_output,) = step(restore_kernel, [((2 * CELLS, HALF), BF)], [], *v.parts_e)

        def stage_finish_h():
            v.out_c, v.out_e = step(
                finish_hidden_kernel, [((HALF * 3, 128), F32), ((BLOCK, WIDTH), F32)], [],
                v.mine_h, v.other_h,
            )

        def stage_joined_s():
            (mine,) = step(
                joined_sum_kernel, [((rows_j + 16, HALF), BF)],
                [((GROUP, rows_j, HALF), BF), ((GROUP, 16, HALF), F32)], *v.parts_j
            )
            v.mine_j = swap_rest(mine)
            v.other_j = swap(v.mine_j)

        def stage_restore_w():
            (v.input_gradient,) = step(
                restore_wide_kernel, [((6 * CELLS, 128), F32)], [((2 * CELLS, HALF), F32)], *v.parts_j
            )

        def stage_finish_j():
            v.out_q, v.out_o, v.out_hidden, v.out_heads, v.out_table, *v.rows = step(
                finish_joined_kernel,
                [((BLOCK // 2 * 9, 128), F32), ((BLOCK // 2 * 3, 128), F32), ((1, WIDTH), F32),
                 ((2, BLOCK), F32), ((HEADS, REL), F32)] + [((1, BLOCK), F32)] * 6,
                [((2 * SMALL, HALF), F32), ((8, WIDTH), F32)],
                v.mine_j, v.other_j,
            )

        stage_order()
        stage_bias()
        stage_unpack()
        stage_half()
        stage_stack()
        stage_pass()
        stage_couple()
        stage_first()
        stage_attend()
        stage_expand_w()
        stage_contract_w()
        stage_couple_att()
        stage_expand()
        stage_contract_g()
        stage_hidden()
        stage_half_sum()
        stage_expand_g()
        stage_cross()
        stage_out_sum()
        stage_attend_b()
        stage_joined()
        stage_contract_s()
        stage_expand_p()
        stage_in_sum()
        stage_rows()
        stage_expand_s()
        stage_joined_p()
        stage_restore()
        stage_finish_h()
        stage_joined_s()
        stage_restore_w()
        stage_finish_j()
        rows = [row.reshape(BLOCK) for row in v.rows]
        return (
            v.layer_output.reshape(inputs.shape),
            v.input_gradient.reshape(inputs.shape),
            rows[4],
            rows[5],
            v.out_q.reshape(query_key_value.shape),
            v.out_heads,
            v.out_table.T,
            v.out_o.reshape(output_weight.shape),
            rows[1],
            rows[2],
            rows[3],
            v.out_e,
            v.out_hidden.reshape(WIDTH),
            v.out_c.reshape(contract_weight.shape),
            rows[0],
        )

    return local


def solution(mesh):
    in_specs = (
        P(("dp", "col"), "row", None),
        P(("dp", "col"), "row", None),
        P(),
        P(),
        P(),
        P("row"),
        P("row"),
        P("row", None, "col", None),
        P(None, "col"),
        P(None, "col"),
        P("col", "row", None),
        P("row"),
        P("row"),
        P("row"),
        P("row", "col"),
        P("col"),
        P("col", "row", None),
        P("row"),
    )
    out_specs = (
        P(("dp", "col"), "row", None),
        P(("dp", "col"), "row", None),
        P("row"),
        P("row"),
        P("row", None, "col", None),
        P(None, "col"),
        P(None, "col"),
        P("col", "row", None),
        P("row"),
        P("row"),
        P("row"),
        P("row", "col"),
        P("col"),
        P("col", "row", None),
        P("row"),
    )
    local = local_program(mesh.shape["dp"], mesh.shape["row"], mesh.shape["col"])
    return jax.shard_map(local, mesh=mesh, in_specs=in_specs, out_specs=out_specs, check_vma=False)
```

```python
import types

import jax
import jax.numpy as jnp
from jax import lax
from jax.experimental import pallas as pl
from jax.experimental.pallas import tpu as pltpu
from jax.sharding import PartitionSpec as P

HEAD_DIM = 32
SIDE = 24
WIN = 12
SHIFT = 6
REL = 529
CELLS = WIN * WIN
NORM_EPS = 1e-05
MASK_FILL = -100.0
BF = jnp.bfloat16
F32 = jnp.float32
NT = (((1,), (1,)), ((), ()))
TN = (((0,), (0,)), ((), ()))
BLOCK = 192
WIDTH = 768
HALF = 384
GROUP = 4
TOKENS = GROUP * CELLS
HEADS = BLOCK // HEAD_DIM
STACK_TAKES = False
VMEM_MIB = 24
ORDER_MIB = 60
ROOT_HALF = 0.7071067811865476
ROOT_TWO_PI_INV = 0.3989422804014327


def dot(a, b):
    return jnp.dot(a, b, preferred_element_type=F32)


def dot_nt(a, b):
    return lax.dot_general(a, b, NT, preferred_element_type=F32)


def dot_tn(a, b):
    return lax.dot_general(a, b, TN, preferred_element_type=F32)


def iota(shape, dim):
    return lax.broadcasted_iota(jnp.int32, shape, dim)


def aligned(value, step):
    return pl.multiple_of(value, step)


MICROS = 10


def cost_of(kernel):
    micros = 0.01 if kernel in CHEAP else MICROS
    return pl.CostEstimate(flops=int(micros * 1.1e9), bytes_accessed=int(micros * 3.6e6), transcendentals=0)


def run(kernel, outs, scratch, *arrays, scalars=(), mib=VMEM_MIB, after=()):
    vmem = pl.BlockSpec(memory_space=pltpu.VMEM)
    smem = pl.BlockSpec(memory_space=pltpu.SMEM)
    anywhere = pl.BlockSpec(memory_space=pl.ANY)
    given = len(scalars) + len(arrays)
    made = given + len(after) + len(outs)

    def body(*refs):
        dp = lax.axis_index("dp")
        ids = (dp % 2, lax.axis_index("row"), lax.axis_index("col"), dp)
        kernel(ids, *refs[:given], *refs[given + len(after) : made], *refs[made + 1 :])
        refs[made][...] = jnp.zeros(refs[made].shape, F32)

    return pl.pallas_call(
        body,
        out_shape=[jax.ShapeDtypeStruct(shape, dtype) for shape, dtype in (*outs, ((8, 128), F32))],
        in_specs=[smem] * len(scalars) + [vmem] * len(arrays) + [anywhere] * len(after),
        out_specs=[vmem] * (len(outs) + 1),
        scratch_shapes=[pltpu.VMEM(shape, dtype) for shape, dtype in scratch],
        compiler_params=pltpu.CompilerParams(vmem_limit_bytes=mib * 1024 * 1024),
        cost_estimate=cost_of(kernel),
        name=kernel.__name__,
    )(*scalars, *arrays, *after)


def place(window, position):
    row = (position * 171) >> 11
    col = position - row * WIN
    row = row + (window // 2) * WIN + SHIFT
    col = col + (window % 2) * WIN + SHIFT
    row = jnp.where(row >= SIDE, row - SIDE, row)
    col = jnp.where(col >= SIDE, col - SIDE, col)
    token = row * SIDE + col
    return token >> 1, token & 1


LINES = CELLS // 2
FIRST = 2 * CELLS // 2 + 16
QUARTER = BLOCK // 4
STACK = HEADS * CELLS + 32
CHUNKS = ((0, 256), (256, 256), (512, 256), (768, 128))
ATT = 2 * CELLS


def order_kernel(
    ids, g0, g1, g2, g3, g4, g5, paired, cotangent, joined, out_own, o0, o1, o2, o3, held, vectors
):
    for n, vector in enumerate((g0, g1, g2, g3, g4, g5)):
        vectors[n : n + 1, :] = vector[...]
    z = ids[1]
    count = paired.shape[0]
    picks = []
    for s in range(GROUP):
        half, parity = place((z + s) % GROUP, iota((CELLS, count), 0))
        hit = half == iota((CELLS, count), 1)
        picks.append([jnp.where(hit & (parity == q), 1.0, 0.0).astype(BF) for q in range(2)])
    even, odd = [jnp.concatenate([pick[q] for pick in picks], axis=0) for q in range(2)]
    rows = [dot(even, v[:, :BLOCK]) + dot(odd, v[:, BLOCK:]) for v in (paired, cotangent)]
    whole = vectors[...]
    high = whole.astype(BF).astype(F32)
    rest = whole - high
    middle = rest.astype(BF).astype(F32)
    begin = aligned(ids[0] * QUARTER, 16)
    for s, out in enumerate((o0, o1, o2, o3)):
        held[s, 2 * LINES :, :] = jnp.zeros((FIRST - 2 * LINES, HALF), F32)
        held[s, 2 * LINES : 2 * LINES + 6, :BLOCK] = high
        held[s, 2 * LINES : 2 * LINES + 6, BLOCK:] = middle
        held[s, 2 * LINES + 8 : 2 * LINES + 14, :BLOCK] = rest - middle
        for n in range(2):
            for k in range(2):
                held[s, n * LINES : (n + 1) * LINES, k * BLOCK : (k + 1) * BLOCK] = rows[n][
                    s * CELLS + k * LINES : s * CELLS + (k + 1) * LINES
                ]
        out[0:FIRST, :] = held[s].astype(BF)
        for part in range(3):
            out[FIRST + part * QUARTER : FIRST + (part + 1) * QUARTER, :] = joined[part, pl.ds(begin, QUARTER), :]
        out[FIRST + 3 * QUARTER :, :] = out_own[pl.ds(begin, QUARTER), :]


def unpack_kernel(ids, slots, a, b, c, d, tokens, vectors, stack):
    flag = slots[ids[3] * GROUP + ids[2]] != 0
    vectors[...] = jnp.zeros(vectors.shape, F32)
    for s, piece in enumerate((a, b, c, d)):
        lanes = slice(s * BLOCK, (s + 1) * BLOCK)
        whole = piece[0:FIRST, :].astype(F32)
        for n in range(2):
            part = whole[n * LINES : (n + 1) * LINES]
            part = jnp.concatenate([part[:, :BLOCK], part[:, BLOCK:]], axis=0)
            if n == 1:
                part = jnp.where(flag, part, jnp.zeros_like(part))
            tokens[n * CELLS : (n + 1) * CELLS, lanes] = part.astype(BF)
        line = 2 * LINES
        vectors[0:6, lanes] = (
            whole[line : line + 6, :BLOCK] + whole[line : line + 6, BLOCK:] + whole[line + 8 : line + 14, :BLOCK]
        )
        if s > 0:
            stack[s - 1] = piece[FIRST:, :]


def couple_kernel(ids, a, b, out):
    out[0] = a[...]
    out[1] = b[...]


def couple_out_kernel(ids, a, b, out):
    couple_kernel(ids, a, b, out)


def couple_att_kernel(ids, a, b, out):
    couple_kernel(ids, a, b, out)


def half_kernel(ids, whole, out):
    rows = out.shape[0]
    out[...] = whole[pl.ds(aligned(ids[0] * rows, 16), rows), :]


def pass_kernel(ids, whole, out):
    out[...] = whole[...]


def stack_kernel(ids, a, b, c, out):
    for s, piece in enumerate((a, b, c)):
        out[s] = piece[...]


def restore_halves(ids, pieces):
    z = ids[1]
    count = SIDE * SIDE // 2
    even = odd = None
    for s in range(GROUP):
        half, parity = place((z + s) % GROUP, iota((count, CELLS), 1))
        hit = half == iota((count, CELLS), 0)
        pick_even = jnp.where(hit & (parity == 0), 1.0, 0.0).astype(BF)
        pick_odd = jnp.where(hit & (parity == 1), 1.0, 0.0).astype(BF)
        piece = pieces[s]
        more_even = dot(pick_even, piece)
        more_odd = dot(pick_odd, piece)
        even = more_even if even is None else even + more_even
        odd = more_odd if odd is None else odd + more_odd
    return even, odd


def restore_kernel(ids, a, b, c, d, out):
    even, odd = restore_halves(ids, [window_piece(v[v.shape[0] - EXTRA :, :]) for v in (a, b, c, d)])
    out[:, :BLOCK] = even.astype(BF)
    out[:, BLOCK:] = odd.astype(BF)


def restore_wide_kernel(ids, a, b, c, d, out, whole):
    even, odd = restore_halves(ids, [window_piece(v[v.shape[0] - EXTRA :, :]) for v in (a, b, c, d)])
    whole[:, :BLOCK] = even
    whole[:, BLOCK:] = odd
    count = whole.shape[0]
    for k in range(3):
        out[pl.ds(k, count, stride=3), :] = whole[:, k * 128 : (k + 1) * 128]


def pair_picks(rows):
    low = iota((rows, rows // 2), 0)
    high = iota((rows, rows // 2), 1)
    pick_even = jnp.where(low == 2 * high, 1.0, 0.0).astype(BF)
    pick_odd = jnp.where(low == 2 * high + 1, 1.0, 0.0).astype(BF)
    return pick_even, pick_odd


def hidden_perm():
    natural = iota((WIDTH, WIDTH), 0)
    split = iota((WIDTH, WIDTH), 1)
    wanted = jnp.where(split < HALF, 2 * split, 2 * split - (WIDTH - 1))
    return jnp.where(natural == wanted, 1.0, 0.0).astype(BF)


def put_halves(ids, held, s, where, rows, mine, other):
    x = ids[0]
    held[(s, *where, pl.ds(aligned(x * rows, 16), rows), slice(None))] = mine
    held[(s, *where, pl.ds(aligned((1 - x) * rows, 16), rows), slice(None))] = other


def first_weights_kernel(ids, own, own_out, mine, other, out, out_square, held):
    pick_even, pick_odd = pair_picks(BLOCK)
    for part in range(4):
        held[0, part] = own[part] if part < 3 else own_out[...]
        lines = slice(part * QUARTER, (part + 1) * QUARTER)
        for s in range(1, GROUP):
            put_halves(ids, held, s, (part,), QUARTER, mine[s - 1, lines, :], other[s - 1, lines, :])
    for s in range(GROUP):
        for part in range(4):
            block = (dot(pick_even, held[s, part, :, :BLOCK]) + dot(pick_odd, held[s, part, :, BLOCK:])).astype(BF)
            if part < 3:
                out[part, s * BLOCK : (s + 1) * BLOCK, :] = block
            else:
                out_square[:, s * BLOCK : (s + 1) * BLOCK] = block


def expand_weights_kernel(ids, own, mine, other, bias, out, out_bias, held, rows):
    perm = hidden_perm()
    held[0] = own[...]
    for s in range(1, GROUP):
        put_halves(ids, held, s, (), BLOCK // 2, mine[s - 1], other[s - 1])
    for s in range(GROUP):
        out[s * BLOCK : (s + 1) * BLOCK, :] = dot(held[s], perm).astype(BF)
    high = bias[...].astype(BF).astype(F32)
    rest = bias[...] - high
    middle = rest.astype(BF).astype(F32)
    rows[...] = jnp.zeros(rows.shape, F32)
    rows[0:1, :] = high
    rows[1:2, :] = middle
    rows[2:3, :] = rest - middle
    found = dot(rows[...].astype(BF), perm)
    out_bias[...] = found[0:1] + found[1:2] + found[2:3]


def contract_weights_kernel(ids, own, m1, m2, m3, out):
    for s, piece in enumerate((own, m1, m2, m3)):
        for q in range(2):
            out[q * HALF : (q + 1) * HALF, s * BLOCK : (s + 1) * BLOCK] = piece[:, q * BLOCK : (q + 1) * BLOCK]


def entry_hits(offset, index):
    row = offset[pl.ds(index, 1), :]
    return jnp.where(iota((REL, CELLS), 0) == row, 1.0, 0.0).astype(BF)


STRIP = 3 * 128
FAR = WIN - 1
SPAN = FAR * WIN


def lane_col():
    lane = iota((8, STRIP), 1)
    return lane - ((lane * 171) >> 11) * WIN


def bias_kernel(ids, table, offset, labels, labels_t, out, parts, strips, mask):
    z = ids[1]
    parts[...] = jnp.zeros(parts.shape, F32)
    whole = table[...]
    high = whole.astype(BF).astype(F32)
    rest = whole - high
    middle = rest.astype(BF).astype(F32)
    parts[0:HEADS, :] = high
    parts[8 : 8 + HEADS, :] = middle
    parts[16 : 16 + HEADS, :] = rest - middle
    split = parts[...].astype(BF)
    row_label = labels[pl.ds(z, 1), :]
    col_label = jnp.sum(jnp.where(iota((CELLS, GROUP), 1) == z, labels_t[...], 0), axis=1, keepdims=True)
    mask[...] = jnp.where(row_label == col_label, 0.0, MASK_FILL)
    sides = []
    for c in (FAR, 0):
        rows = []
        for r in (FAR, 0):
            found = dot(split, entry_hits(offset, r * WIN + c))
            rows.append((found[0:8] + found[8:16]) + found[16:24])
        sides.append(
            jnp.concatenate([rows[0], rows[1][:, WIN:], jnp.zeros((8, STRIP - CELLS - SPAN), F32)], axis=1)
        )
    col = lane_col()
    for c in range(WIN):
        near = pltpu.roll(sides[0], (STRIP - (FAR - c)) % STRIP, 1)
        far = pltpu.roll(sides[1], c, 1)
        strips[c] = jnp.where(col <= c, near, far)
    for h in range(HEADS):
        strip = strips[:, h, :]
        for r in range(WIN):
            begin = (FAR - r) * WIN
            out[r * WIN : (r + 1) * WIN, h * CELLS : (h + 1) * CELLS] = (
                strip[:, begin : begin + CELLS] + mask[r * WIN : (r + 1) * WIN, :]
            )
    out[:, HEADS * CELLS :] = jnp.zeros((CELLS, STACK - HEADS * CELLS), F32)


def table_sums(grads, offset, strips, wide):
    for h in range(HEADS):
        wide[h] = jnp.zeros(wide.shape[1:], F32)
        for r in range(WIN):
            begin = (FAR - r) * WIN
            wide[h, :, begin : begin + CELLS] += grads[r * WIN : (r + 1) * WIN, h * CELLS : (h + 1) * CELLS]
        strips[:, h, :] = wide[h]
    col = lane_col()
    zero = jnp.zeros((8, STRIP), F32)
    near = far = zero
    for c in range(WIN):
        strip = strips[c]
        near = near + pltpu.roll(jnp.where(col <= c, strip, zero), FAR - c, 1)
        far = far + pltpu.roll(jnp.where(col <= c, zero, strip), (STRIP - c) % STRIP, 1)
    total = None
    for c, side in ((FAR, near), (0, far)):
        upper = side[:, 0:CELLS]
        lower = jnp.concatenate([jnp.zeros((8, WIN), F32), side[:, CELLS : CELLS + SPAN]], axis=1)
        for r, piece in ((FAR, upper), (0, lower)):
            high = piece.astype(BF).astype(F32)
            both = jnp.concatenate([high, piece - high], axis=0).astype(BF)
            found = dot_nt(both, entry_hits(offset, r * WIN + c))
            total = found if total is None else total + found
    return total[0:8] + total[8:16]


def norm_stats(values):
    centre = jnp.mean(values, axis=-1, keepdims=True)
    moved = values - centre
    inverse = lax.rsqrt(jnp.mean(moved * moved, axis=-1, keepdims=True) + NORM_EPS)
    return moved * inverse, inverse


def turned(block):
    return block.astype(F32).T.astype(BF)


def stack_heads(block, lane_head, out):
    for h in range(HEADS):
        out[h * CELLS : (h + 1) * CELLS, :] = jnp.where(lane_head == h, block, jnp.zeros_like(block))
    out[HEADS * CELLS :, :] = jnp.zeros((STACK - HEADS * CELLS, BLOCK), BF)


def pick_heads(wide, held):
    for h in range(HEADS):
        lines = slice(h * HEAD_DIM, (h + 1) * HEAD_DIM)
        held[lines, :] = wide[lines, h * CELLS : (h + 1) * CELLS]
    return held[...].T


def attend_kernel(ids, *refs):
    pieces = refs[0:2]
    vectors, weights, head_bias, bias = refs[2:6]
    tokens, normed, queries, keys, values, probs, attended = refs[6:13]
    stacked, held = refs[13:15]
    gain = vectors[0:1, :]
    shift = vectors[1:2, :]
    for j in range(GROUP):
        tokens[j * CELLS : (j + 1) * CELLS, :] = pieces[j & 1][j >> 1, 0:CELLS, :]

    @pl.loop(0, GROUP)
    def _(w):
        rows = pl.ds(aligned(w * CELLS, 16), CELLS)
        scaled, _ = norm_stats(tokens[rows, :].astype(F32))
        normed[rows, :] = (scaled * gain + shift).astype(BF)

    scale = float(HEAD_DIM) ** (-0.5)
    whole = normed[...]
    queries[...] = ((dot(whole, weights[0]) + head_bias[0:1, :]) * scale).astype(BF)
    keys[...] = dot(whole, weights[1]).astype(BF)
    values[...] = (dot(whole, weights[2]) + head_bias[1:2, :]).astype(BF)
    lane_head = iota((CELLS, BLOCK), 1) // HEAD_DIM
    for w in range(GROUP):
        rows = pl.ds(w * CELLS, CELLS)
        key = keys[rows, :]
        stack_heads(queries[rows, :], lane_head, stacked.at[w])
        for begin, count in CHUNKS:
            scores = dot_nt(key, stacked[w, begin : begin + count, :]) + bias[:, begin : begin + count]
            powers = jnp.exp(scores - jnp.max(scores, axis=0, keepdims=True))
            share = powers * (1.0 / jnp.sum(powers, axis=0, keepdims=True))
            probs[w, :, begin : begin + count] = share.astype(BF)
        total = pick_heads(dot(turned(values[rows, :]), probs[w]), held.at[w])
        attended[(w & 1) * CELLS : (w & 1) * CELLS + CELLS, (w >> 1) * BLOCK : (w >> 1) * BLOCK + BLOCK] = (
            total.astype(BF)
        )


def expand_kernel(ids, *refs):
    tokens = refs[0]
    attended = refs[1:3]
    out_weights = refs[3:5]
    vectors, weights, hidden_bias = refs[5:8]
    middle, normed, hidden, slope = refs[8:12]
    joined, square = refs[12:14]
    for j in range(GROUP):
        square[j * BLOCK : (j + 1) * BLOCK, :] = out_weights[j & 1][j >> 1]
        for i in range(GROUP):
            k = i ^ j
            joined[i * CELLS : (i + 1) * CELLS, j * BLOCK : (j + 1) * BLOCK] = attended[j & 1][
                j >> 1, (k & 1) * CELLS : (k & 1) * CELLS + CELLS, (k >> 1) * BLOCK : (k >> 1) * BLOCK + BLOCK
            ]
    out_bias = vectors[2:3, :]
    gain = vectors[3:4, :]
    shift = vectors[4:5, :]

    @pl.loop(0, 2)
    def _(t):
        rows = pl.ds(aligned(t * (TOKENS // 2), 16), TOKENS // 2)
        mid = tokens[rows, :].astype(F32) + dot(joined[rows, :], square[...]) + out_bias
        middle[rows, :] = mid
        scaled, _ = norm_stats(mid)
        second = (scaled * gain + shift).astype(BF)
        normed[rows, :] = second
        pre = dot(second, weights[...]) + hidden_bias[...]
        bell = 0.5 * (1.0 + lax.erf(pre * ROOT_HALF))
        hidden[rows, :] = (pre * bell).astype(BF)
        slope[rows, :] = bell + pre * (ROOT_TWO_PI_INV * jnp.exp(-0.5 * pre * pre))


def split_slots(product, keep, send):
    keep[0:CELLS, :] = product[0:CELLS].astype(keep.dtype)
    keep[CELLS : 2 * CELLS, :] = product[2 * CELLS : 3 * CELLS].astype(keep.dtype)
    send[0:CELLS, :] = product[CELLS : 2 * CELLS].astype(send.dtype)
    send[CELLS : 2 * CELLS, :] = product[3 * CELLS :].astype(send.dtype)


def hidden_back_kernel(ids, u0, u1, contract, slope, expand, upstream, pre_grad, keep, send):
    for j in range(GROUP):
        upstream[j * CELLS : (j + 1) * CELLS, :] = (u0, u1)[j & 1][j >> 1, CELLS:, :]
    pre_grad[...] = (dot_nt(upstream[...], contract[...]) * slope[...]).astype(BF)
    split_slots(dot_nt(pre_grad[...], expand[...]), keep, send)


def contract_grads_kernel(ids, u0, u1, hidden, o0, o1, o2, o3, upstream):
    for j in range(GROUP):
        upstream[j * CELLS : (j + 1) * CELLS, :] = (u0, u1)[j & 1][j >> 1, CELLS:, :]
    up = upstream[...]
    for q in range(2):
        block = dot_tn(hidden[:, q * HALF : (q + 1) * HALF], up).astype(BF)
        for s, out in enumerate((o0, o1, o2, o3)):
            out[:, q * BLOCK : (q + 1) * BLOCK] = block[:, s * BLOCK : (s + 1) * BLOCK]


def expand_grads_kernel(
    ids, upstream, hidden, normed, pre_grad, contract, keep, send, keep_out, send_out, sums, whole_e,
):
    x = ids[0]
    mixed = dot_tn(normed[...], pre_grad[...]).astype(BF)
    perm = hidden_perm()
    whole_e[...] = dot_nt(mixed, perm).astype(BF)
    lines = BLOCK // 2
    for s in range(GROUP):
        for out, side in ((keep, x), (send, 1 - x)):
            out[s] = whole_e[pl.ds(aligned(s * BLOCK + side * lines, 16), lines), :]
    split_slots(dot(hidden[...], contract[...]), keep_out, send_out)
    sums[...] = jnp.zeros(sums.shape, F32)
    total = jnp.sum(pre_grad[...].astype(F32), axis=0, keepdims=True)
    high = total.astype(BF).astype(F32)
    middle = (total - high).astype(BF).astype(F32)
    sums[0:1, :] = high
    sums[1:2, :] = middle
    sums[2:3, :] = total - high - middle
    found = dot_nt(sums[...].astype(BF), perm)
    sums[0:1, :] = found[0:1] + found[1:2] + found[2:3]
    sums[1:2, :] = jnp.sum(upstream[0:CELLS, :].astype(F32), axis=0, keepdims=True)


def attend_back_kernel(ids, *refs):
    even_total, odd_total, middle, upstream = refs[0:4]
    vectors, out_weights, queries, keys, values, probs, weights = refs[4:11]
    tokens, hidden_sums = refs[11:13]
    own_mid, mid_low, joined, bias_grad, keep, send = refs[13:19]
    attended_grad, stacked, stacked_grad, scores, held, sums = refs[19:25]
    gain = vectors[3:4, :]
    sums[...] = jnp.zeros(sums.shape, F32)
    for w in range(GROUP):
        rows = pl.ds(w * CELLS, CELLS)
        source = (even_total, odd_total)[w & 1]
        grad = source[(w >> 1) * CELLS : (w >> 1) * CELLS + CELLS, :].astype(F32)
        scaled, inverse = norm_stats(middle[rows, :])
        e = grad * gain
        part = e - jnp.mean(e, axis=-1, keepdims=True) - scaled * jnp.mean(e * scaled, axis=-1, keepdims=True)
        mid = upstream[rows, :].astype(F32) + inverse * part
        low = mid.astype(BF)
        mid_low[rows, :] = low
        if w == 0:
            own_mid[...] = mid
            sums[0:1, :] = hidden_sums[1:2, :]
            sums[1:2, :] = jnp.sum(low.astype(F32), axis=0, keepdims=True)
            sums[2:3, :] = jnp.sum(grad * scaled, axis=0, keepdims=True)
            sums[3:4, :] = jnp.sum(grad, axis=0, keepdims=True)
    attended_grad[...] = dot_nt(mid_low[...], out_weights[...]).astype(BF)
    lane_head = iota((CELLS, BLOCK), 1) // HEAD_DIM
    scale = float(HEAD_DIM) ** (-0.5)
    for w in range(GROUP):
        rows = pl.ds(w * CELLS, CELLS)
        key = keys[rows, :]
        value = values[rows, :]
        stack_heads(queries[rows, :], lane_head, stacked.at[w])
        stack_heads(attended_grad[rows, :], lane_head, stacked_grad.at[w])
        for begin, count in CHUNKS:
            lanes = slice(begin, begin + count)
            share = probs[w, :, lanes].astype(F32)
            product = share * dot_nt(value, stacked_grad[w, lanes, :])
            score = (product - share * jnp.sum(product, axis=0, keepdims=True)).astype(BF)
            scores[w, :, lanes] = score
            if w == 0:
                bias_grad[:, lanes] = score.astype(F32)
            else:
                bias_grad[:, lanes] += score.astype(F32)
        value_grad = dot(probs[w], stacked_grad[w])
        key_grad = dot(scores[w], stacked[w])
        query_grad = pick_heads(dot(turned(key), scores[w]), held.at[w])
        joined[0, rows, :] = (query_grad * scale).astype(BF)
        joined[1, rows, :] = key_grad.astype(BF)
        joined[2, rows, :] = value_grad.astype(BF)
    product = dot_nt(joined[0], weights[0]) + dot_nt(joined[1], weights[1]) + dot_nt(joined[2], weights[2])
    split_slots(product, keep, send)
    gains = shifts = None
    for w in range(GROUP):
        grad = product[w * CELLS : (w + 1) * CELLS]
        scaled, _ = norm_stats(tokens[w * CELLS : (w + 1) * CELLS, :].astype(F32))
        more_gains = jnp.sum(grad * scaled, axis=0, keepdims=True)
        more_shifts = jnp.sum(grad, axis=0, keepdims=True)
        gains = more_gains if gains is None else gains + more_gains
        shifts = more_shifts if shifts is None else shifts + more_shifts
    sums[4:5, :] = gains
    sums[5:6, :] = shifts
    low = sums[...].astype(BF)
    keep[2 * CELLS :, :] = low.astype(F32)
    send[2 * CELLS :, :] = low


SMALL = 16


def joined_grads_kernel(
    ids, normed, joined, attended, mid_low, hidden_sums,
    bias_grad, offset, keep, send, whole_q, whole_o, small, small_low, strips, strip_sums,
):
    x = ids[0]
    whole = normed[...]
    picks = pair_picks(BLOCK)
    for part in range(3):
        natural = dot_tn(whole, joined[part]).astype(BF)
        for s in range(GROUP):
            for q in range(2):
                whole_q[part, s * (BLOCK // 2) : (s + 1) * (BLOCK // 2), q * BLOCK : (q + 1) * BLOCK] = dot_tn(
                    picks[q], natural[s * BLOCK : (s + 1) * BLOCK]
                ).astype(BF)
    low = mid_low[...]
    total = None
    for k in range(2):
        left = attended[0:ATT, k * BLOCK : (k + 1) * BLOCK]
        product = dot_tn(left, low[2 * k * CELLS : (2 * k + 2) * CELLS])
        total = product if total is None else total + product
    wide = total.astype(BF)
    for q in range(2):
        lines = dot_tn(picks[q], wide).astype(BF)
        for s in range(GROUP):
            whole_o[s, :, q * BLOCK : (q + 1) * BLOCK] = lines[:, s * BLOCK : (s + 1) * BLOCK]
    small[...] = jnp.zeros(small.shape, F32)
    table = table_sums(bias_grad, offset, strips, strip_sums)
    for s in range(GROUP):
        small[s, 0:1, :] = hidden_sums[0:1, :HALF]
        small[s, 1:2, :] = hidden_sums[0:1, HALF:]
        for part in range(3):
            small[s, 2 + part : 3 + part, 0:BLOCK] = jnp.sum(joined[part].astype(F32), axis=0, keepdims=True)
        small[s, 5 : 5 + HEADS, :] = table[0:HEADS, 0:HALF]
        small[s, 11 : 11 + HEADS, 0 : REL - HALF] = table[0:HEADS, HALF:REL]
    small_low[...] = small[...].astype(BF)
    rows = BLOCK // 4
    for s in range(GROUP):
        begin = s * (BLOCK // 2)
        for out, side in ((keep, x), (send, 1 - x)):
            for part in range(3):
                out[s, part * rows : (part + 1) * rows, :] = whole_q[part, pl.ds(aligned(begin + side * rows, 16), rows), :]
            out[s, 3 * rows : 4 * rows, :] = whole_o[s, pl.ds(aligned(side * rows, 16), rows), :]
            out[s, 4 * rows :, :] = small_low[s, pl.ds(aligned(side * SMALL, 16), SMALL), :]


EXTRA = 80


def window_lines(result, s, held):
    lanes = slice(s * BLOCK, (s + 1) * BLOCK)
    held[s, 0:LINES, :BLOCK] = result[0:LINES, lanes]
    held[s, 0:LINES, BLOCK:] = result[LINES:, lanes]
    held[s, LINES:, :] = jnp.zeros((EXTRA - LINES, HALF), F32)


def window_piece(lines):
    whole = lines.astype(F32)
    return jnp.concatenate([whole[0:LINES, :BLOCK], whole[0:LINES, BLOCK:]], axis=0).astype(BF)


def expand_pack_kernel(ids, keep, came, middle, pair, came_out, vectors, o0, o1, o2, o3, held):
    total = pair[0:CELLS, :].astype(F32) + came_out[...].astype(F32)
    result = middle[0:CELLS, :] + total + vectors[5:6, :]
    lines = BLOCK // 2
    for s, out in enumerate((o0, o1, o2, o3)):
        both = keep[s].astype(F32) + came[s].astype(F32)
        out[0:lines, :] = both[:, :HALF].astype(BF)
        out[lines : 2 * lines, :] = both[:, HALF:].astype(BF)
        window_lines(result, s, held)
        out[2 * lines :, :] = held[s].astype(BF)


def joined_pack_kernel(ids, keep, came, pair, came_in, tokens, own_mid, vectors, o0, o1, o2, o3, held):
    total = pair[0:CELLS, :].astype(F32) + came_in[0:CELLS, :].astype(F32)
    scaled, inverse = norm_stats(tokens[0:CELLS, :].astype(F32))
    e = total * vectors[0:1, :]
    part = e - jnp.mean(e, axis=-1, keepdims=True) - scaled * jnp.mean(e * scaled, axis=-1, keepdims=True)
    result = own_mid[...] + inverse * part
    totals = (pair[2 * CELLS :, :].astype(F32) + came_in[CELLS:, :].astype(F32))[0:8]
    rows = keep.shape[1]
    for s, out in enumerate((o0, o1, o2, o3)):
        out[0:rows, :] = (keep[s].astype(F32) + came[s].astype(F32)).astype(BF)
        window_lines(result, s, held)
        held[s, LINES:, :BLOCK] = totals[:, s * BLOCK : (s + 1) * BLOCK]
        out[rows:, :] = held[s].astype(BF)


def ordered_sum(ids, pieces, rows, held):
    z = ids[1]
    for s, piece in enumerate(pieces):
        held[(z + s) % GROUP] = piece[0:rows, :]
    return (
        ((held[0].astype(F32) + held[1].astype(F32)) + held[2].astype(F32)) + held[3].astype(F32)
    ).astype(BF)


def ordered_sum_kernel(ids, a, b, c, d, out, held):
    out[...] = ordered_sum(ids, (a, b, c, d), out.shape[0], held)


def joined_sum_kernel(ids, a, b, c, d, out, held, lines):
    rows = held.shape[1]
    pieces = (a, b, c, d)
    out[0:rows, :] = ordered_sum(ids, pieces, rows, held)
    for s, piece in enumerate(pieces):
        lines[(ids[1] + s) % GROUP] = piece[rows + EXTRA - 16 :, :].astype(F32)
    out[rows:, :] = (((lines[0] + lines[1]) + lines[2]) + lines[3]).astype(BF)


def expand_sum_kernel(ids, mine_c, a, b, c, d, out, held):
    out[0:HALF, :] = mine_c[...]
    out[HALF:, :] = ordered_sum(ids, (a, b, c, d), BLOCK, held)


def half_sum_kernel(ids, keep, came, out):
    out[...] = (keep[...] + came[...].astype(F32)).astype(BF)


def input_sum_kernel(ids, keep, came, out):
    half_sum_kernel(ids, keep, came, out)


def cross_sum_kernel(ids, kept, came, out):
    for k in range(2):
        mine = slice(k * CELLS, (k + 1) * CELLS)
        theirs = slice((1 - k) * CELLS, (2 - k) * CELLS)
        out[mine, :] = (kept[mine, :].astype(F32) + came[theirs, :].astype(F32)).astype(BF)


def wide_store(out, piece, begin, step, offset):
    count = piece.shape[0]
    for k in range(3):
        out[pl.ds(begin * step + offset + k, count, stride=step), :] = piece[:, k * 128 : (k + 1) * 128]


def finish_hidden_kernel(ids, mine, other, out_c, out_e):
    x = ids[0]
    wide_store(out_c, mine[0:HALF, :].astype(F32) + other[0:HALF, :].astype(F32), 0, 3, 0)
    lines = BLOCK // 2
    for piece, side in ((mine, x), (other, 1 - x)):
        for k in range(2):
            out_e[pl.ds(aligned(side * lines, 8), lines), k * HALF : (k + 1) * HALF] = piece[
                HALF + k * lines : HALF + (k + 1) * lines, :
            ].astype(F32)


def finish_joined_kernel(ids, mine, other, out_q, out_o, out_hidden, out_heads, out_table, r0, r1, r2, r3, r4, r5, small):
    x = ids[0]
    for piece, side in ((mine, x), (other, 1 - x)):
        for part in range(3):
            wide_store(out_q, piece[part * QUARTER : (part + 1) * QUARTER, :].astype(F32), side * QUARTER, 9, part * 3)
        wide_store(out_o, piece[3 * QUARTER : 4 * QUARTER, :].astype(F32), side * QUARTER, 3, 0)
        small[pl.ds(aligned(side * SMALL, 8), SMALL), :] = piece[4 * QUARTER : 4 * QUARTER + SMALL, :].astype(F32)
    for k in range(6):
        out_hidden[k : k + 1, :] = small[k // 3 : k // 3 + 1, (k % 3) * 128 : (k % 3 + 1) * 128]
    out_heads[0:1, :] = small[2:3, :BLOCK]
    out_heads[1:2, :] = small[4:5, :BLOCK]
    out_table[:, :HALF] = small[5 : 5 + HEADS, :]
    out_table[:, HALF:] = small[11 : 11 + HEADS, 0 : REL - HALF]
    ends = []
    for piece in (mine, other):
        ends.append(piece[4 * QUARTER + SMALL :, :BLOCK].astype(F32)[8:16])
    total = ends[0] + ends[1]
    for n, out in enumerate((r0, r1, r2, r3, r4, r5)):
        out[...] = total[n : n + 1]


CHEAP = (couple_kernel, first_weights_kernel, pass_kernel, attend_kernel, expand_weights_kernel, couple_out_kernel, couple_att_kernel, ordered_sum_kernel, expand_pack_kernel)


def local_program(dp_size, row_size, col_size):
    def turn(value, shift):
        return lax.ppermute(value, "row", [(i, (i + shift) % row_size) for i in range(row_size)])

    def flip(value, bits):
        return lax.ppermute(value, "col", [(i, i ^ bits) for i in range(col_size)])

    def swap(value, bits=1):
        return lax.ppermute(value, "dp", [(i, i ^ bits) for i in range(dp_size)])

    def swap_rest(value):
        bits = 2
        while bits < dp_size:
            value = (value.astype(F32) + swap(value, bits).astype(F32)).astype(value.dtype)
            bits *= 2
        return value

    def turn_all(value):
        return [turn(value, s) for s in range(1, row_size)]

    def give_back(slots):
        return [slots[0]] + [turn(slots[s], -s) for s in range(1, row_size)]

    def local(
        inputs, cotangent, slot_mask, region_ids, offset_index, first_gain, first_shift,
        query_key_value, query_value_bias, position_table, output_weight, output_bias,
        second_gain, second_shift, expand_weight, expand_bias, contract_weight, contract_bias,
    ):
        joined_own = query_key_value.reshape(BLOCK // 2, 3, HALF).transpose(1, 0, 2)
        out_own = output_weight.reshape(BLOCK // 2, HALF)
        contract_own = contract_weight.reshape(HALF, HALF)
        vectors_own = [
            vector.reshape(1, BLOCK)
            for vector in (first_gain, first_shift, output_bias, second_gain, second_shift, contract_bias)
        ]
        last = []

        def step(kernel, outs, scratch, *arrays, **given):
            results = run(kernel, outs, scratch, *arrays, after=tuple(last), **given)
            last[:] = [results[-1]]
            return results[:-1]

        v = types.SimpleNamespace()
        two = (2 * CELLS, WIDTH)
        more = (2 * CELLS + 16, WIDTH)
        wide = (TOKENS, WIDTH)
        rows_j = BLOCK + SMALL

        def stage_order():
            slots = step(
                order_kernel, [((FIRST + BLOCK, HALF), BF)] * GROUP, [((GROUP, FIRST, HALF), F32), ((6, BLOCK), F32)],
                *vectors_own, inputs.reshape(2 * CELLS, HALF), cotangent.reshape(2 * CELLS, HALF),
                joined_own, out_own, mib=ORDER_MIB,
            )
            v.slots = [slots[0]] + [turn(slots[s], s) for s in range(1, row_size)]

        def stage_bias():
            labels = region_ids.reshape(2, WIN, 2, WIN).transpose(0, 2, 1, 3).reshape(GROUP, CELLS)
            (v.bias,) = step(
                bias_kernel, [((CELLS, STACK), F32)],
                [((24, REL), F32), ((WIN, 8, STRIP), F32), ((CELLS, CELLS), F32)],
                position_table.T, offset_index.T, labels, labels.T,
            )

        def stage_unpack():
            v.own, v.vectors, v.first = step(
                unpack_kernel, [(two, BF), ((8, WIDTH), F32), ((3, BLOCK, HALF), BF)], [],
                *v.slots, scalars=(slot_mask,),
            )
            v.first_other = swap(v.first)
            v.across = flip(v.own, 2)

        def stage_half():
            (half,) = step(half_kernel, [((BLOCK // 2, WIDTH), BF)], [], expand_weight)
            v.expand_mine = turn_all(half)

        def stage_stack():
            last.extend(v.tokens[1:] if STACK_TAKES else ())
            (v.expand,) = step(stack_kernel, [((3, BLOCK // 2, WIDTH), BF)], [], *v.expand_mine)
            v.expand_other = swap(v.expand)

        def stage_couple():
            (both,) = step(couple_kernel, [((2, *two), BF)], [], v.own, v.across)
            v.tokens = (both, flip(both, 1))

        def stage_first():
            v.joined_w, v.out_w = step(
                first_weights_kernel, [((3, WIDTH, BLOCK), BF), ((BLOCK, WIDTH), BF)],
                [((GROUP, 4, BLOCK // 2, HALF), BF)], joined_own, out_own, v.first, v.first_other,
            )

            v.out_across = flip(v.out_w, 2)

        def stage_couple_ow():
            (both,) = step(couple_out_kernel, [((2, BLOCK, WIDTH), BF)], [], v.out_w, v.out_across)
            v.out_square = (both, flip(both, 1))

        def stage_pass():
            (passed,) = step(pass_kernel, [((HALF, HALF), BF)], [], contract_own)
            v.contract = turn_all(passed)

        def stage_attend():
            v.x, v.n1, v.q, v.k, v.v, v.p, v.att = step(
                attend_kernel,
                [(wide, BF)] * 2 + [((TOKENS, BLOCK), BF)] * 3
                + [((GROUP, CELLS, STACK), BF), ((ATT, HALF), BF)],
                [((GROUP, STACK, BLOCK), BF), ((GROUP, BLOCK, CELLS), F32)], *v.tokens, v.vectors, v.joined_w, query_value_bias, v.bias,
            )
            v.att_across = flip(v.att, 2)

        def stage_expand_w():
            v.expand_w, v.hidden_bias = step(
                expand_weights_kernel, [((WIDTH, WIDTH), BF), ((1, WIDTH), F32)],
                [((GROUP, BLOCK, WIDTH), BF), ((8, WIDTH), F32)],
                expand_weight, v.expand, v.expand_other, expand_bias.reshape(1, WIDTH),
            )

        def stage_couple_att():
            (both,) = step(couple_att_kernel, [((2, ATT, HALF), BF)], [], v.att, v.att_across)
            v.attended = (both, flip(both, 1))

        def stage_expand():
            v.middle, v.n2, v.hidden, v.slope = step(
                expand_kernel, [(wide, F32), (wide, BF), (wide, BF), (wide, F32)],
                [(wide, BF), ((WIDTH, WIDTH), BF)],
                v.x, *v.attended, *v.out_square, v.vectors, v.expand_w, v.hidden_bias,
            )

        def stage_contract_g():
            parts = step(
                contract_grads_kernel, [((HALF, HALF), BF)] * GROUP, [(wide, BF)], *v.tokens, v.hidden
            )
            v.parts_c = give_back(parts)

        def stage_contract_w():
            (v.contract_w,) = step(
                contract_weights_kernel, [((WIDTH, WIDTH), BF)], [], contract_own, *v.contract
            )

        def stage_hidden():
            v.up, v.pre, v.keep_n, send = step(
                hidden_back_kernel, [(wide, BF)] * 2 + [(two, F32), (two, BF)], [],
                *v.tokens, v.contract_w, v.slope, v.expand_w,
            )
            v.came_n = flip(send, 1)

        def stage_half_sum():
            (v.even,) = step(half_sum_kernel, [(two, BF)], [], v.keep_n, v.came_n)
            v.even_came = flip(v.even, 2)

        def stage_expand_g():
            v.keep_e, send_e, v.keep_out, send_out, v.hidden_sums = step(
                expand_grads_kernel,
                [((GROUP, BLOCK // 2, WIDTH), BF)] * 2 + [(two, F32), (two, BF), ((8, WIDTH), F32)],
                [((WIDTH, WIDTH), BF)],
                v.up, v.hidden, v.n2, v.pre, v.contract_w,
            )
            v.came_e = swap(send_e)
            v.came_out = flip(send_out, 1)

        def stage_cross():
            (v.even_total,) = step(cross_sum_kernel, [(two, BF)], [], v.even, v.even_came)
            v.odd_total = flip(v.even_total, 1)

        def stage_out_sum():
            (v.pair_out,) = step(half_sum_kernel, [(two, BF)], [], v.keep_out, v.came_out)
            v.far_out = flip(v.pair_out[CELLS:], 2)

        def stage_attend_b():
            v.own_mid, v.mid_low, v.joined_g, v.bias_g, v.keep_i, send = step(
                attend_back_kernel,
                [((CELLS, WIDTH), F32), (wide, BF), ((3, TOKENS, BLOCK), BF),
                 ((CELLS, STACK), F32), (more, F32), (more, BF)],
                [((TOKENS, BLOCK), BF), ((GROUP, STACK, BLOCK), BF), ((GROUP, STACK, BLOCK), BF),
                 ((GROUP, CELLS, STACK), BF), ((GROUP, BLOCK, CELLS), F32), ((16, WIDTH), F32)],
                v.even_total, v.odd_total, v.middle, v.up, v.vectors, v.out_w,
                v.q, v.k, v.v, v.p, v.joined_w, v.x, v.hidden_sums,
            )
            v.came_i = flip(send, 1)

        def stage_contract_s():
            (v.mine_c,) = step(
                ordered_sum_kernel, [((HALF, HALF), BF)], [((GROUP, HALF, HALF), BF)], *v.parts_c
            )

        def stage_expand_p():
            parts = step(
                expand_pack_kernel, [((BLOCK + EXTRA, HALF), BF)] * GROUP, [((GROUP, EXTRA, HALF), F32)],
                v.keep_e, v.came_e, v.middle, v.pair_out, v.far_out, v.vectors,
            )
            v.parts_e = give_back(parts)

        def stage_in_sum():
            (v.pair_in,) = step(input_sum_kernel, [(more, BF)], [], v.keep_i, v.came_i)
            v.far_in = flip(v.pair_in[CELLS:], 2)

        def stage_joined():
            v.keep_j, send = step(
                joined_grads_kernel, [((GROUP, rows_j, HALF), BF)] * 2,
                [((3, HALF, HALF), BF), ((GROUP, BLOCK // 2, HALF), BF),
                 ((GROUP, 2 * SMALL, HALF), F32), ((GROUP, 2 * SMALL, HALF), BF),
                 ((WIN, 8, STRIP), F32), ((HEADS, WIN, STRIP), F32)],
                v.n1, v.joined_g, v.att, v.mid_low, v.hidden_sums, v.bias_g, offset_index.T,
            )
            v.came_j = swap(send)

        def stage_expand_s():
            (mine,) = step(
                expand_sum_kernel, [((HALF + BLOCK, HALF), BF)], [((GROUP, BLOCK, HALF), BF)],
                v.mine_c, *v.parts_e,
            )
            v.mine_h = swap_rest(mine)
            v.other_h = swap(v.mine_h)

        def stage_joined_p():
            parts = step(
                joined_pack_kernel, [((rows_j + EXTRA, HALF), BF)] * GROUP, [((GROUP, EXTRA, HALF), F32)],
                v.keep_j, v.came_j, v.pair_in, v.far_in, v.x, v.own_mid, v.vectors,
            )
            v.parts_j = give_back(parts)

        def stage_restore():
            (v.layer_output,) = step(restore_kernel, [((2 * CELLS, HALF), BF)], [], *v.parts_e)

        def stage_finish_h():
            v.out_c, v.out_e = step(
                finish_hidden_kernel, [((HALF * 3, 128), F32), ((BLOCK, WIDTH), F32)], [],
                v.mine_h, v.other_h,
            )

        def stage_joined_s():
            (mine,) = step(
                joined_sum_kernel, [((rows_j + 16, HALF), BF)],
                [((GROUP, rows_j, HALF), BF), ((GROUP, 16, HALF), F32)], *v.parts_j
            )
            v.mine_j = swap_rest(mine)
            v.other_j = swap(v.mine_j)

        def stage_restore_w():
            (v.input_gradient,) = step(
                restore_wide_kernel, [((6 * CELLS, 128), F32)], [((2 * CELLS, HALF), F32)], *v.parts_j
            )

        def stage_finish_j():
            v.out_q, v.out_o, v.out_hidden, v.out_heads, v.out_table, *v.rows = step(
                finish_joined_kernel,
                [((BLOCK // 2 * 9, 128), F32), ((BLOCK // 2 * 3, 128), F32), ((6, 128), F32),
                 ((2, BLOCK), F32), ((HEADS, REL), F32)] + [((1, BLOCK), F32)] * 6,
                [((2 * SMALL, HALF), F32)],
                v.mine_j, v.other_j,
            )

        stage_order()
        stage_bias()
        stage_unpack()
        stage_half()
        stage_couple()
        stage_first()
        stage_pass()
        stage_stack()
        stage_attend()
        stage_couple_ow()
        stage_expand_w()
        stage_couple_att()
        stage_contract_w()
        stage_expand()
        stage_contract_g()
        stage_hidden()
        stage_half_sum()
        stage_expand_g()
        stage_cross()
        stage_out_sum()
        stage_attend_b()
        stage_contract_s()
        stage_expand_p()
        stage_joined()
        stage_in_sum()
        stage_expand_s()
        stage_joined_p()
        stage_restore()
        stage_finish_h()
        stage_joined_s()
        stage_restore_w()
        stage_finish_j()
        rows = [row.reshape(BLOCK) for row in v.rows]
        return (
            v.layer_output.reshape(inputs.shape),
            v.input_gradient.reshape(inputs.shape),
            rows[4],
            rows[5],
            v.out_q.reshape(query_key_value.shape),
            v.out_heads,
            v.out_table.T,
            v.out_o.reshape(output_weight.shape),
            rows[1],
            rows[2],
            rows[3],
            v.out_e,
            v.out_hidden.reshape(WIDTH),
            v.out_c.reshape(contract_weight.shape),
            rows[0],
        )

    return local


def solution(mesh):
    in_specs = (
        P(("dp", "col"), "row", None),
        P(("dp", "col"), "row", None),
        P(),
        P(),
        P(),
        P("row"),
        P("row"),
        P("row", None, "col", None),
        P(None, "col"),
        P(None, "col"),
        P("col", "row", None),
        P("row"),
        P("row"),
        P("row"),
        P("row", "col"),
        P("col"),
        P("col", "row", None),
        P("row"),
    )
    out_specs = (
        P(("dp", "col"), "row", None),
        P(("dp", "col"), "row", None),
        P("row"),
        P("row"),
        P("row", None, "col", None),
        P(None, "col"),
        P(None, "col"),
        P("col", "row", None),
        P("row"),
        P("row"),
        P("row"),
        P("row", "col"),
        P("col"),
        P("col", "row", None),
        P("row"),
    )
    local = local_program(mesh.shape["dp"], mesh.shape["row"], mesh.shape["col"])
    return jax.shard_map(local, mesh=mesh, in_specs=in_specs, out_specs=out_specs, check_vma=False)
```

```python
import types

import jax
import jax.numpy as jnp
from jax import lax
from jax.experimental import pallas as pl
from jax.experimental.pallas import tpu as pltpu
from jax.sharding import PartitionSpec as P

HEAD_DIM = 32
SIDE = 24
WIN = 12
SHIFT = 6
REL = 529
CELLS = WIN * WIN
NORM_EPS = 1e-05
MASK_FILL = -100.0
BF = jnp.bfloat16
F32 = jnp.float32
NT = (((1,), (1,)), ((), ()))
TN = (((0,), (0,)), ((), ()))
BLOCK = 192
WIDTH = 768
HALF = 384
GROUP = 4
TOKENS = GROUP * CELLS
HEADS = BLOCK // HEAD_DIM
STACK_TAKES = False
VMEM_MIB = 24
ORDER_MIB = 60
ROOT_HALF = 0.7071067811865476
ROOT_TWO_PI_INV = 0.3989422804014327


def dot(a, b):
    return jnp.dot(a, b, preferred_element_type=F32)


def dot_nt(a, b):
    return lax.dot_general(a, b, NT, preferred_element_type=F32)


def dot_tn(a, b):
    return lax.dot_general(a, b, TN, preferred_element_type=F32)


def iota(shape, dim):
    return lax.broadcasted_iota(jnp.int32, shape, dim)


def aligned(value, step):
    return pl.multiple_of(value, step)


MICROS = 10


def cost_of(kernel):
    micros = 0.01 if kernel in CHEAP else MICROS
    return pl.CostEstimate(flops=int(micros * 1.1e9), bytes_accessed=int(micros * 3.6e6), transcendentals=0)


def run(kernel, outs, scratch, *arrays, scalars=(), mib=VMEM_MIB, after=()):
    vmem = pl.BlockSpec(memory_space=pltpu.VMEM)
    smem = pl.BlockSpec(memory_space=pltpu.SMEM)
    anywhere = pl.BlockSpec(memory_space=pl.ANY)
    given = len(scalars) + len(arrays)
    made = given + len(after) + len(outs)

    def body(*refs):
        dp = lax.axis_index("dp")
        ids = (dp % 2, lax.axis_index("row"), lax.axis_index("col"), dp)
        kernel(ids, *refs[:given], *refs[given + len(after) : made], *refs[made + 1 :])
        refs[made][...] = jnp.zeros(refs[made].shape, F32)

    return pl.pallas_call(
        body,
        out_shape=[jax.ShapeDtypeStruct(shape, dtype) for shape, dtype in (*outs, ((8, 128), F32))],
        in_specs=[smem] * len(scalars) + [vmem] * len(arrays) + [anywhere] * len(after),
        out_specs=[vmem] * (len(outs) + 1),
        scratch_shapes=[pltpu.VMEM(shape, dtype) for shape, dtype in scratch],
        compiler_params=pltpu.CompilerParams(vmem_limit_bytes=mib * 1024 * 1024),
        cost_estimate=cost_of(kernel),
        name=kernel.__name__,
    )(*scalars, *arrays, *after)


def place(window, position):
    row = (position * 171) >> 11
    col = position - row * WIN
    row = row + (window // 2) * WIN + SHIFT
    col = col + (window % 2) * WIN + SHIFT
    row = jnp.where(row >= SIDE, row - SIDE, row)
    col = jnp.where(col >= SIDE, col - SIDE, col)
    token = row * SIDE + col
    return token >> 1, token & 1


LINES = CELLS // 2
FIRST = 2 * CELLS // 2 + 16
QUARTER = BLOCK // 4
STACK = HEADS * CELLS + 32
CHUNKS = ((0, 256), (256, 256), (512, 256), (768, 128))
ATT = 2 * CELLS


def order_kernel(
    ids, g0, g1, g2, g3, g4, g5, paired, cotangent, joined, out_own, o0, o1, o2, o3, held, vectors
):
    for n, vector in enumerate((g0, g1, g2, g3, g4, g5)):
        vectors[n : n + 1, :] = vector[...]
    z = ids[1]
    count = paired.shape[0]
    picks = []
    for s in range(GROUP):
        half, parity = place((z + s) % GROUP, iota((CELLS, count), 0))
        hit = half == iota((CELLS, count), 1)
        picks.append([jnp.where(hit & (parity == q), 1.0, 0.0).astype(BF) for q in range(2)])
    even, odd = [jnp.concatenate([pick[q] for pick in picks], axis=0) for q in range(2)]
    rows = [dot(even, v[:, :BLOCK]) + dot(odd, v[:, BLOCK:]) for v in (paired, cotangent)]
    whole = vectors[...]
    high = whole.astype(BF).astype(F32)
    rest = whole - high
    middle = rest.astype(BF).astype(F32)
    begin = aligned(ids[0] * QUARTER, 16)
    for s, out in enumerate((o0, o1, o2, o3)):
        held[s, 2 * LINES :, :] = jnp.zeros((FIRST - 2 * LINES, HALF), F32)
        held[s, 2 * LINES : 2 * LINES + 6, :BLOCK] = high
        held[s, 2 * LINES : 2 * LINES + 6, BLOCK:] = middle
        held[s, 2 * LINES + 8 : 2 * LINES + 14, :BLOCK] = rest - middle
        for n in range(2):
            for k in range(2):
                held[s, n * LINES : (n + 1) * LINES, k * BLOCK : (k + 1) * BLOCK] = rows[n][
                    s * CELLS + k * LINES : s * CELLS + (k + 1) * LINES
                ]
        out[0:FIRST, :] = held[s].astype(BF)
        for part in range(3):
            out[FIRST + part * QUARTER : FIRST + (part + 1) * QUARTER, :] = joined[part, pl.ds(begin, QUARTER), :]
        out[FIRST + 3 * QUARTER :, :] = out_own[pl.ds(begin, QUARTER), :]


def unpack_kernel(ids, slots, a, b, c, d, tokens, vectors, stack):
    flag = slots[ids[3] * GROUP + ids[2]] != 0
    vectors[...] = jnp.zeros(vectors.shape, F32)
    for s, piece in enumerate((a, b, c, d)):
        lanes = slice(s * BLOCK, (s + 1) * BLOCK)
        whole = piece[0:FIRST, :].astype(F32)
        for n in range(2):
            part = whole[n * LINES : (n + 1) * LINES]
            part = jnp.concatenate([part[:, :BLOCK], part[:, BLOCK:]], axis=0)
            if n == 1:
                part = jnp.where(flag, part, jnp.zeros_like(part))
            tokens[n * CELLS : (n + 1) * CELLS, lanes] = part.astype(BF)
        line = 2 * LINES
        vectors[0:6, lanes] = (
            whole[line : line + 6, :BLOCK] + whole[line : line + 6, BLOCK:] + whole[line + 8 : line + 14, :BLOCK]
        )
        if s > 0:
            stack[s - 1] = piece[FIRST:, :]


def couple_kernel(ids, a, b, out):
    out[0] = a[...]
    out[1] = b[...]


def couple_out_kernel(ids, a, b, out):
    couple_kernel(ids, a, b, out)


def couple_att_kernel(ids, a, b, out):
    couple_kernel(ids, a, b, out)


def half_kernel(ids, whole, out):
    rows = out.shape[0]
    out[...] = whole[pl.ds(aligned(ids[0] * rows, 16), rows), :]


def pass_kernel(ids, whole, out):
    out[...] = whole[...]


def stack_kernel(ids, a, b, c, out):
    for s, piece in enumerate((a, b, c)):
        out[s] = piece[...]


def restore_halves(ids, pieces):
    z = ids[1]
    count = SIDE * SIDE // 2
    even = odd = None
    for s in range(GROUP):
        half, parity = place((z + s) % GROUP, iota((count, CELLS), 1))
        hit = half == iota((count, CELLS), 0)
        pick_even = jnp.where(hit & (parity == 0), 1.0, 0.0).astype(BF)
        pick_odd = jnp.where(hit & (parity == 1), 1.0, 0.0).astype(BF)
        piece = pieces[s]
        more_even = dot(pick_even, piece)
        more_odd = dot(pick_odd, piece)
        even = more_even if even is None else even + more_even
        odd = more_odd if odd is None else odd + more_odd
    return even, odd


def restore_kernel(ids, a, b, c, d, out):
    even, odd = restore_halves(ids, [window_piece(v[v.shape[0] - EXTRA :, :]) for v in (a, b, c, d)])
    out[:, :BLOCK] = even.astype(BF)
    out[:, BLOCK:] = odd.astype(BF)


def restore_wide_kernel(ids, a, b, c, d, out, whole):
    even, odd = restore_halves(ids, [window_piece(v[v.shape[0] - EXTRA :, :]) for v in (a, b, c, d)])
    whole[:, :BLOCK] = even
    whole[:, BLOCK:] = odd
    count = whole.shape[0]
    for k in range(3):
        out[pl.ds(k, count, stride=3), :] = whole[:, k * 128 : (k + 1) * 128]


def pair_picks(rows):
    low = iota((rows, rows // 2), 0)
    high = iota((rows, rows // 2), 1)
    pick_even = jnp.where(low == 2 * high, 1.0, 0.0).astype(BF)
    pick_odd = jnp.where(low == 2 * high + 1, 1.0, 0.0).astype(BF)
    return pick_even, pick_odd


def hidden_perm():
    natural = iota((WIDTH, WIDTH), 0)
    split = iota((WIDTH, WIDTH), 1)
    wanted = jnp.where(split < HALF, 2 * split, 2 * split - (WIDTH - 1))
    return jnp.where(natural == wanted, 1.0, 0.0).astype(BF)


def put_halves(ids, held, s, where, rows, mine, other):
    x = ids[0]
    held[(s, *where, pl.ds(aligned(x * rows, 16), rows), slice(None))] = mine
    held[(s, *where, pl.ds(aligned((1 - x) * rows, 16), rows), slice(None))] = other


def first_weights_kernel(ids, own, own_out, mine, other, out, out_square, held):
    pick_even, pick_odd = pair_picks(BLOCK)
    for part in range(4):
        held[0, part] = own[part] if part < 3 else own_out[...]
        lines = slice(part * QUARTER, (part + 1) * QUARTER)
        for s in range(1, GROUP):
            put_halves(ids, held, s, (part,), QUARTER, mine[s - 1, lines, :], other[s - 1, lines, :])
    for s in range(GROUP):
        for part in range(4):
            block = (dot(pick_even, held[s, part, :, :BLOCK]) + dot(pick_odd, held[s, part, :, BLOCK:])).astype(BF)
            if part < 3:
                out[part, s * BLOCK : (s + 1) * BLOCK, :] = block
            else:
                out_square[:, s * BLOCK : (s + 1) * BLOCK] = block


def expand_weights_kernel(ids, own, mine, other, bias, out, out_bias, held, rows):
    perm = hidden_perm()
    held[0] = own[...]
    for s in range(1, GROUP):
        put_halves(ids, held, s, (), BLOCK // 2, mine[s - 1], other[s - 1])
    for s in range(GROUP):
        out[s * BLOCK : (s + 1) * BLOCK, :] = dot(held[s], perm).astype(BF)
    high = bias[...].astype(BF).astype(F32)
    rest = bias[...] - high
    middle = rest.astype(BF).astype(F32)
    rows[...] = jnp.zeros(rows.shape, F32)
    rows[0:1, :] = high
    rows[1:2, :] = middle
    rows[2:3, :] = rest - middle
    found = dot(rows[...].astype(BF), perm)
    out_bias[...] = found[0:1] + found[1:2] + found[2:3]


def contract_weights_kernel(ids, own, m1, m2, m3, out):
    for s, piece in enumerate((own, m1, m2, m3)):
        for q in range(2):
            out[q * HALF : (q + 1) * HALF, s * BLOCK : (s + 1) * BLOCK] = piece[:, q * BLOCK : (q + 1) * BLOCK]


def entry_hits(offset, index):
    row = offset[pl.ds(index, 1), :]
    return jnp.where(iota((REL, CELLS), 0) == row, 1.0, 0.0).astype(BF)


STRIP = 3 * 128
FAR = WIN - 1
SPAN = FAR * WIN


def lane_col():
    lane = iota((8, STRIP), 1)
    return lane - ((lane * 171) >> 11) * WIN


def bias_kernel(ids, table, offset, labels, labels_t, out, parts, strips, mask):
    z = ids[1]
    parts[...] = jnp.zeros(parts.shape, F32)
    whole = table[...]
    high = whole.astype(BF).astype(F32)
    rest = whole - high
    middle = rest.astype(BF).astype(F32)
    parts[0:HEADS, :] = high
    parts[8 : 8 + HEADS, :] = middle
    parts[16 : 16 + HEADS, :] = rest - middle
    split = parts[...].astype(BF)
    row_label = labels[pl.ds(z, 1), :]
    col_label = jnp.sum(jnp.where(iota((CELLS, GROUP), 1) == z, labels_t[...], 0), axis=1, keepdims=True)
    mask[...] = jnp.where(row_label == col_label, 0.0, MASK_FILL)
    sides = []
    for c in (FAR, 0):
        rows = []
        for r in (FAR, 0):
            found = dot(split, entry_hits(offset, r * WIN + c))
            rows.append((found[0:8] + found[8:16]) + found[16:24])
        sides.append(
            jnp.concatenate([rows[0], rows[1][:, WIN:], jnp.zeros((8, STRIP - CELLS - SPAN), F32)], axis=1)
        )
    col = lane_col()
    for c in range(WIN):
        near = pltpu.roll(sides[0], (STRIP - (FAR - c)) % STRIP, 1)
        far = pltpu.roll(sides[1], c, 1)
        strips[c] = jnp.where(col <= c, near, far)
    for h in range(HEADS):
        strip = strips[:, h, :]
        for r in range(WIN):
            begin = (FAR - r) * WIN
            out[r * WIN : (r + 1) * WIN, h * CELLS : (h + 1) * CELLS] = (
                strip[:, begin : begin + CELLS] + mask[r * WIN : (r + 1) * WIN, :]
            )
    out[:, HEADS * CELLS :] = jnp.zeros((CELLS, STACK - HEADS * CELLS), F32)


def table_sums(grads, offset, strips, wide):
    for h in range(HEADS):
        wide[h] = jnp.zeros(wide.shape[1:], F32)
        for r in range(WIN):
            begin = (FAR - r) * WIN
            wide[h, :, begin : begin + CELLS] += grads[r * WIN : (r + 1) * WIN, h * CELLS : (h + 1) * CELLS]
        strips[:, h, :] = wide[h]
    col = lane_col()
    zero = jnp.zeros((8, STRIP), F32)
    near = far = zero
    for c in range(WIN):
        strip = strips[c]
        near = near + pltpu.roll(jnp.where(col <= c, strip, zero), FAR - c, 1)
        far = far + pltpu.roll(jnp.where(col <= c, zero, strip), (STRIP - c) % STRIP, 1)
    total = None
    for c, side in ((FAR, near), (0, far)):
        upper = side[:, 0:CELLS]
        lower = jnp.concatenate([jnp.zeros((8, WIN), F32), side[:, CELLS : CELLS + SPAN]], axis=1)
        for r, piece in ((FAR, upper), (0, lower)):
            high = piece.astype(BF).astype(F32)
            both = jnp.concatenate([high, piece - high], axis=0).astype(BF)
            found = dot_nt(both, entry_hits(offset, r * WIN + c))
            total = found if total is None else total + found
    return total[0:8] + total[8:16]


def norm_stats(values):
    centre = jnp.mean(values, axis=-1, keepdims=True)
    moved = values - centre
    inverse = lax.rsqrt(jnp.mean(moved * moved, axis=-1, keepdims=True) + NORM_EPS)
    return moved * inverse, inverse


def turned(block):
    return block.astype(F32).T.astype(BF)


def stack_heads(block, lane_head, out):
    for h in range(HEADS):
        out[h * CELLS : (h + 1) * CELLS, :] = jnp.where(lane_head == h, block, jnp.zeros_like(block))
    out[HEADS * CELLS :, :] = jnp.zeros((STACK - HEADS * CELLS, BLOCK), BF)


def pick_heads(wide, held):
    for h in range(HEADS):
        lines = slice(h * HEAD_DIM, (h + 1) * HEAD_DIM)
        held[lines, :] = wide[lines, h * CELLS : (h + 1) * CELLS]
    return held[...].T


def attend_kernel(ids, *refs):
    pieces = refs[0:2]
    vectors, weights, head_bias, bias = refs[2:6]
    tokens, normed, queries, keys, values, probs, attended = refs[6:13]
    stacked, held = refs[13:15]
    gain = vectors[0:1, :]
    shift = vectors[1:2, :]
    for j in range(GROUP):
        tokens[j * CELLS : (j + 1) * CELLS, :] = pieces[j & 1][j >> 1, 0:CELLS, :]

    @pl.loop(0, GROUP)
    def _(w):
        rows = pl.ds(aligned(w * CELLS, 16), CELLS)
        scaled, _ = norm_stats(tokens[rows, :].astype(F32))
        normed[rows, :] = (scaled * gain + shift).astype(BF)

    scale = float(HEAD_DIM) ** (-0.5)
    whole = normed[...]
    queries[...] = ((dot(whole, weights[0]) + head_bias[0:1, :]) * scale).astype(BF)
    keys[...] = dot(whole, weights[1]).astype(BF)
    values[...] = (dot(whole, weights[2]) + head_bias[1:2, :]).astype(BF)
    lane_head = iota((CELLS, BLOCK), 1) // HEAD_DIM
    for w in range(GROUP):
        rows = pl.ds(w * CELLS, CELLS)
        key = keys[rows, :]
        stack_heads(queries[rows, :], lane_head, stacked.at[w])
        for begin, count in CHUNKS:
            scores = dot_nt(key, stacked[w, begin : begin + count, :]) + bias[:, begin : begin + count]
            powers = jnp.exp(scores - jnp.max(scores, axis=0, keepdims=True))
            share = powers * (1.0 / jnp.sum(powers, axis=0, keepdims=True))
            probs[w, :, begin : begin + count] = share.astype(BF)
        total = pick_heads(dot(turned(values[rows, :]), probs[w]), held.at[w])
        attended[(w & 1) * CELLS : (w & 1) * CELLS + CELLS, (w >> 1) * BLOCK : (w >> 1) * BLOCK + BLOCK] = (
            total.astype(BF)
        )


def expand_kernel(ids, *refs):
    tokens = refs[0]
    attended = refs[1:3]
    out_weights = refs[3:5]
    vectors, weights, hidden_bias = refs[5:8]
    middle, normed, hidden, slope = refs[8:12]
    joined, square = refs[12:14]
    for j in range(GROUP):
        square[j * BLOCK : (j + 1) * BLOCK, :] = out_weights[j & 1][j >> 1]
        for i in range(GROUP):
            k = i ^ j
            joined[i * CELLS : (i + 1) * CELLS, j * BLOCK : (j + 1) * BLOCK] = attended[j & 1][
                j >> 1, (k & 1) * CELLS : (k & 1) * CELLS + CELLS, (k >> 1) * BLOCK : (k >> 1) * BLOCK + BLOCK
            ]
    out_bias = vectors[2:3, :]
    gain = vectors[3:4, :]
    shift = vectors[4:5, :]

    @pl.loop(0, 2)
    def _(t):
        rows = pl.ds(aligned(t * (TOKENS // 2), 16), TOKENS // 2)
        mid = tokens[rows, :].astype(F32) + dot(joined[rows, :], square[...]) + out_bias
        middle[rows, :] = mid
        scaled, _ = norm_stats(mid)
        second = (scaled * gain + shift).astype(BF)
        normed[rows, :] = second
        pre = dot(second, weights[...]) + hidden_bias[...]
        bell = 0.5 * (1.0 + lax.erf(pre * ROOT_HALF))
        hidden[rows, :] = (pre * bell).astype(BF)
        slope[rows, :] = bell + pre * (ROOT_TWO_PI_INV * jnp.exp(-0.5 * pre * pre))


def split_slots(product, keep, send):
    keep[0:CELLS, :] = product[0:CELLS].astype(keep.dtype)
    keep[CELLS : 2 * CELLS, :] = product[2 * CELLS : 3 * CELLS].astype(keep.dtype)
    send[0:CELLS, :] = product[CELLS : 2 * CELLS].astype(send.dtype)
    send[CELLS : 2 * CELLS, :] = product[3 * CELLS :].astype(send.dtype)


def hidden_back_kernel(ids, u0, u1, contract, slope, expand, upstream, pre_grad, keep, send):
    for j in range(GROUP):
        upstream[j * CELLS : (j + 1) * CELLS, :] = (u0, u1)[j & 1][j >> 1, CELLS:, :]
    pre_grad[...] = (dot_nt(upstream[...], contract[...]) * slope[...]).astype(BF)
    split_slots(dot_nt(pre_grad[...], expand[...]), keep, send)


def contract_grads_kernel(ids, u0, u1, hidden, o0, o1, o2, o3, upstream):
    for j in range(GROUP):
        upstream[j * CELLS : (j + 1) * CELLS, :] = (u0, u1)[j & 1][j >> 1, CELLS:, :]
    up = upstream[...]
    for q in range(2):
        block = dot_tn(hidden[:, q * HALF : (q + 1) * HALF], up).astype(BF)
        for s, out in enumerate((o0, o1, o2, o3)):
            out[:, q * BLOCK : (q + 1) * BLOCK] = block[:, s * BLOCK : (s + 1) * BLOCK]


def expand_grads_kernel(
    ids, upstream, hidden, normed, pre_grad, contract, keep, send, keep_out, send_out, sums, whole_e,
):
    x = ids[0]
    mixed = dot_tn(normed[...], pre_grad[...]).astype(BF)
    perm = hidden_perm()
    whole_e[...] = dot_nt(mixed, perm).astype(BF)
    lines = BLOCK // 2
    for s in range(GROUP):
        for out, side in ((keep, x), (send, 1 - x)):
            out[s] = whole_e[pl.ds(aligned(s * BLOCK + side * lines, 16), lines), :]
    split_slots(dot(hidden[...], contract[...]), keep_out, send_out)
    sums[...] = jnp.zeros(sums.shape, F32)
    total = jnp.sum(pre_grad[...].astype(F32), axis=0, keepdims=True)
    high = total.astype(BF).astype(F32)
    middle = (total - high).astype(BF).astype(F32)
    sums[0:1, :] = high
    sums[1:2, :] = middle
    sums[2:3, :] = total - high - middle
    found = dot_nt(sums[...].astype(BF), perm)
    sums[0:1, :] = found[0:1] + found[1:2] + found[2:3]
    sums[1:2, :] = jnp.sum(upstream[0:CELLS, :].astype(F32), axis=0, keepdims=True)


def expand_both_kernel(ids, *refs):
    expand_kernel(ids, *refs[0:8], *refs[10:14], *refs[18:20])
    contract_grads_kernel(ids, *refs[8:10], refs[12], *refs[14:18], refs[20])


def attend_back_kernel(ids, *refs):
    even_total, odd_total, middle, upstream = refs[0:4]
    vectors, out_weights, queries, keys, values, probs, weights = refs[4:11]
    tokens, hidden_sums = refs[11:13]
    own_mid, mid_low, joined, bias_grad, keep, send = refs[13:19]
    attended_grad, stacked, stacked_grad, scores, held, sums = refs[19:25]
    gain = vectors[3:4, :]
    sums[...] = jnp.zeros(sums.shape, F32)
    for w in range(GROUP):
        rows = pl.ds(w * CELLS, CELLS)
        source = (even_total, odd_total)[w & 1]
        grad = source[(w >> 1) * CELLS : (w >> 1) * CELLS + CELLS, :].astype(F32)
        scaled, inverse = norm_stats(middle[rows, :])
        e = grad * gain
        part = e - jnp.mean(e, axis=-1, keepdims=True) - scaled * jnp.mean(e * scaled, axis=-1, keepdims=True)
        mid = upstream[rows, :].astype(F32) + inverse * part
        low = mid.astype(BF)
        mid_low[rows, :] = low
        if w == 0:
            own_mid[...] = mid
            sums[0:1, :] = hidden_sums[1:2, :]
            sums[1:2, :] = jnp.sum(low.astype(F32), axis=0, keepdims=True)
            sums[2:3, :] = jnp.sum(grad * scaled, axis=0, keepdims=True)
            sums[3:4, :] = jnp.sum(grad, axis=0, keepdims=True)
    attended_grad[...] = dot_nt(mid_low[...], out_weights[...]).astype(BF)
    lane_head = iota((CELLS, BLOCK), 1) // HEAD_DIM
    scale = float(HEAD_DIM) ** (-0.5)
    for w in range(GROUP):
        rows = pl.ds(w * CELLS, CELLS)
        key = keys[rows, :]
        value = values[rows, :]
        stack_heads(queries[rows, :], lane_head, stacked.at[w])
        stack_heads(attended_grad[rows, :], lane_head, stacked_grad.at[w])
        for begin, count in CHUNKS:
            lanes = slice(begin, begin + count)
            share = probs[w, :, lanes].astype(F32)
            product = share * dot_nt(value, stacked_grad[w, lanes, :])
            score = (product - share * jnp.sum(product, axis=0, keepdims=True)).astype(BF)
            scores[w, :, lanes] = score
            if w == 0:
                bias_grad[:, lanes] = score.astype(F32)
            else:
                bias_grad[:, lanes] += score.astype(F32)
        value_grad = dot(probs[w], stacked_grad[w])
        key_grad = dot(scores[w], stacked[w])
        query_grad = pick_heads(dot(turned(key), scores[w]), held.at[w])
        joined[0, rows, :] = (query_grad * scale).astype(BF)
        joined[1, rows, :] = key_grad.astype(BF)
        joined[2, rows, :] = value_grad.astype(BF)
    product = dot_nt(joined[0], weights[0]) + dot_nt(joined[1], weights[1]) + dot_nt(joined[2], weights[2])
    split_slots(product, keep, send)
    gains = shifts = None
    for w in range(GROUP):
        grad = product[w * CELLS : (w + 1) * CELLS]
        scaled, _ = norm_stats(tokens[w * CELLS : (w + 1) * CELLS, :].astype(F32))
        more_gains = jnp.sum(grad * scaled, axis=0, keepdims=True)
        more_shifts = jnp.sum(grad, axis=0, keepdims=True)
        gains = more_gains if gains is None else gains + more_gains
        shifts = more_shifts if shifts is None else shifts + more_shifts
    sums[4:5, :] = gains
    sums[5:6, :] = shifts
    low = sums[...].astype(BF)
    keep[2 * CELLS :, :] = low.astype(F32)
    send[2 * CELLS :, :] = low


SMALL = 16


def joined_grads_kernel(
    ids, normed, joined, attended, mid_low, hidden_sums,
    bias_grad, offset, keep, send, whole_q, whole_o, small, small_low, strips, strip_sums,
):
    x = ids[0]
    whole = normed[...]
    picks = pair_picks(BLOCK)
    for part in range(3):
        natural = dot_tn(whole, joined[part]).astype(BF)
        for s in range(GROUP):
            for q in range(2):
                whole_q[part, s * (BLOCK // 2) : (s + 1) * (BLOCK // 2), q * BLOCK : (q + 1) * BLOCK] = dot_tn(
                    picks[q], natural[s * BLOCK : (s + 1) * BLOCK]
                ).astype(BF)
    low = mid_low[...]
    total = None
    for k in range(2):
        left = attended[0:ATT, k * BLOCK : (k + 1) * BLOCK]
        product = dot_tn(left, low[2 * k * CELLS : (2 * k + 2) * CELLS])
        total = product if total is None else total + product
    wide = total.astype(BF)
    for q in range(2):
        lines = dot_tn(picks[q], wide).astype(BF)
        for s in range(GROUP):
            whole_o[s, :, q * BLOCK : (q + 1) * BLOCK] = lines[:, s * BLOCK : (s + 1) * BLOCK]
    small[...] = jnp.zeros(small.shape, F32)
    table = table_sums(bias_grad, offset, strips, strip_sums)
    for s in range(GROUP):
        small[s, 0:1, :] = hidden_sums[0:1, :HALF]
        small[s, 1:2, :] = hidden_sums[0:1, HALF:]
        for part in range(3):
            small[s, 2 + part : 3 + part, 0:BLOCK] = jnp.sum(joined[part].astype(F32), axis=0, keepdims=True)
        small[s, 5 : 5 + HEADS, :] = table[0:HEADS, 0:HALF]
        small[s, 11 : 11 + HEADS, 0 : REL - HALF] = table[0:HEADS, HALF:REL]
    small_low[...] = small[...].astype(BF)
    rows = BLOCK // 4
    for s in range(GROUP):
        begin = s * (BLOCK // 2)
        for out, side in ((keep, x), (send, 1 - x)):
            for part in range(3):
                out[s, part * rows : (part + 1) * rows, :] = whole_q[part, pl.ds(aligned(begin + side * rows, 16), rows), :]
            out[s, 3 * rows : 4 * rows, :] = whole_o[s, pl.ds(aligned(side * rows, 16), rows), :]
            out[s, 4 * rows :, :] = small_low[s, pl.ds(aligned(side * SMALL, 16), SMALL), :]


EXTRA = 80


def window_lines(result, s, held):
    lanes = slice(s * BLOCK, (s + 1) * BLOCK)
    held[s, 0:LINES, :BLOCK] = result[0:LINES, lanes]
    held[s, 0:LINES, BLOCK:] = result[LINES:, lanes]
    held[s, LINES:, :] = jnp.zeros((EXTRA - LINES, HALF), F32)


def window_piece(lines):
    whole = lines.astype(F32)
    return jnp.concatenate([whole[0:LINES, :BLOCK], whole[0:LINES, BLOCK:]], axis=0).astype(BF)


def expand_pack_kernel(ids, keep, came, middle, pair, came_out, vectors, o0, o1, o2, o3, held):
    total = pair[0:CELLS, :].astype(F32) + came_out[...].astype(F32)
    result = middle[0:CELLS, :] + total + vectors[5:6, :]
    lines = BLOCK // 2
    for s, out in enumerate((o0, o1, o2, o3)):
        both = keep[s].astype(F32) + came[s].astype(F32)
        out[0:lines, :] = both[:, :HALF].astype(BF)
        out[lines : 2 * lines, :] = both[:, HALF:].astype(BF)
        window_lines(result, s, held)
        out[2 * lines :, :] = held[s].astype(BF)


def joined_pack_kernel(ids, keep, came, pair, came_in, tokens, own_mid, vectors, o0, o1, o2, o3, held):
    total = pair[0:CELLS, :].astype(F32) + came_in[0:CELLS, :].astype(F32)
    scaled, inverse = norm_stats(tokens[0:CELLS, :].astype(F32))
    e = total * vectors[0:1, :]
    part = e - jnp.mean(e, axis=-1, keepdims=True) - scaled * jnp.mean(e * scaled, axis=-1, keepdims=True)
    result = own_mid[...] + inverse * part
    totals = (pair[2 * CELLS :, :].astype(F32) + came_in[CELLS:, :].astype(F32))[0:8]
    rows = keep.shape[1]
    for s, out in enumerate((o0, o1, o2, o3)):
        out[0:rows, :] = (keep[s].astype(F32) + came[s].astype(F32)).astype(BF)
        window_lines(result, s, held)
        held[s, LINES:, :BLOCK] = totals[:, s * BLOCK : (s + 1) * BLOCK]
        out[rows:, :] = held[s].astype(BF)


def ordered_sum(ids, pieces, rows, held):
    z = ids[1]
    for s, piece in enumerate(pieces):
        held[(z + s) % GROUP] = piece[0:rows, :]
    return (
        ((held[0].astype(F32) + held[1].astype(F32)) + held[2].astype(F32)) + held[3].astype(F32)
    ).astype(BF)


def ordered_sum_kernel(ids, a, b, c, d, out, held):
    out[...] = ordered_sum(ids, (a, b, c, d), out.shape[0], held)


def joined_sum_kernel(ids, a, b, c, d, out, held, lines):
    rows = held.shape[1]
    pieces = (a, b, c, d)
    out[0:rows, :] = ordered_sum(ids, pieces, rows, held)
    for s, piece in enumerate(pieces):
        lines[(ids[1] + s) % GROUP] = piece[rows + EXTRA - 16 :, :].astype(F32)
    out[rows:, :] = (((lines[0] + lines[1]) + lines[2]) + lines[3]).astype(BF)


def expand_sum_kernel(ids, mine_c, a, b, c, d, out, held):
    out[0:HALF, :] = mine_c[...]
    out[HALF:, :] = ordered_sum(ids, (a, b, c, d), BLOCK, held)


def half_sum_kernel(ids, keep, came, out):
    out[...] = (keep[...] + came[...].astype(F32)).astype(BF)


def input_sum_kernel(ids, keep, came, out):
    half_sum_kernel(ids, keep, came, out)


def cross_sum_kernel(ids, kept, came, out):
    for k in range(2):
        mine = slice(k * CELLS, (k + 1) * CELLS)
        theirs = slice((1 - k) * CELLS, (2 - k) * CELLS)
        out[mine, :] = (kept[mine, :].astype(F32) + came[theirs, :].astype(F32)).astype(BF)


def wide_store(out, piece, begin, step, offset):
    count = piece.shape[0]
    for k in range(3):
        out[pl.ds(begin * step + offset + k, count, stride=step), :] = piece[:, k * 128 : (k + 1) * 128]


def finish_hidden_kernel(ids, mine, other, out_c, out_e):
    x = ids[0]
    wide_store(out_c, mine[0:HALF, :].astype(F32) + other[0:HALF, :].astype(F32), 0, 3, 0)
    lines = BLOCK // 2
    for piece, side in ((mine, x), (other, 1 - x)):
        for k in range(2):
            out_e[pl.ds(aligned(side * lines, 8), lines), k * HALF : (k + 1) * HALF] = piece[
                HALF + k * lines : HALF + (k + 1) * lines, :
            ].astype(F32)


def finish_joined_kernel(ids, mine, other, out_q, out_o, out_hidden, out_heads, out_table, r0, r1, r2, r3, r4, r5, small):
    x = ids[0]
    for piece, side in ((mine, x), (other, 1 - x)):
        for part in range(3):
            wide_store(out_q, piece[part * QUARTER : (part + 1) * QUARTER, :].astype(F32), side * QUARTER, 9, part * 3)
        wide_store(out_o, piece[3 * QUARTER : 4 * QUARTER, :].astype(F32), side * QUARTER, 3, 0)
        small[pl.ds(aligned(side * SMALL, 8), SMALL), :] = piece[4 * QUARTER : 4 * QUARTER + SMALL, :].astype(F32)
    for k in range(6):
        out_hidden[k : k + 1, :] = small[k // 3 : k // 3 + 1, (k % 3) * 128 : (k % 3 + 1) * 128]
    out_heads[0:1, :] = small[2:3, :BLOCK]
    out_heads[1:2, :] = small[4:5, :BLOCK]
    out_table[:, :HALF] = small[5 : 5 + HEADS, :]
    out_table[:, HALF:] = small[11 : 11 + HEADS, 0 : REL - HALF]
    ends = []
    for piece in (mine, other):
        ends.append(piece[4 * QUARTER + SMALL :, :BLOCK].astype(F32)[8:16])
    total = ends[0] + ends[1]
    for n, out in enumerate((r0, r1, r2, r3, r4, r5)):
        out[...] = total[n : n + 1]


CHEAP = (couple_kernel, first_weights_kernel, pass_kernel, attend_kernel, expand_weights_kernel, couple_out_kernel, couple_att_kernel, ordered_sum_kernel, expand_pack_kernel)


def local_program(dp_size, row_size, col_size):
    def turn(value, shift):
        return lax.ppermute(value, "row", [(i, (i + shift) % row_size) for i in range(row_size)])

    def flip(value, bits):
        return lax.ppermute(value, "col", [(i, i ^ bits) for i in range(col_size)])

    def swap(value, bits=1):
        return lax.ppermute(value, "dp", [(i, i ^ bits) for i in range(dp_size)])

    def swap_rest(value):
        bits = 2
        while bits < dp_size:
            value = (value.astype(F32) + swap(value, bits).astype(F32)).astype(value.dtype)
            bits *= 2
        return value

    def turn_all(value):
        return [turn(value, s) for s in range(row_size - 1, 0, -1)][::-1]

    def give_back(slots):
        return [slots[0]] + [turn(slots[s], -s) for s in range(row_size - 1, 0, -1)][::-1]

    def local(
        inputs, cotangent, slot_mask, region_ids, offset_index, first_gain, first_shift,
        query_key_value, query_value_bias, position_table, output_weight, output_bias,
        second_gain, second_shift, expand_weight, expand_bias, contract_weight, contract_bias,
    ):
        joined_own = query_key_value.reshape(BLOCK // 2, 3, HALF).transpose(1, 0, 2)
        out_own = output_weight.reshape(BLOCK // 2, HALF)
        contract_own = contract_weight.reshape(HALF, HALF)
        vectors_own = [
            vector.reshape(1, BLOCK)
            for vector in (first_gain, first_shift, output_bias, second_gain, second_shift, contract_bias)
        ]
        last = []

        def step(kernel, outs, scratch, *arrays, **given):
            results = run(kernel, outs, scratch, *arrays, after=tuple(last), **given)
            last[:] = [results[-1]]
            return results[:-1]

        v = types.SimpleNamespace()
        two = (2 * CELLS, WIDTH)
        more = (2 * CELLS + 16, WIDTH)
        wide = (TOKENS, WIDTH)
        rows_j = BLOCK + SMALL

        def stage_order():
            slots = step(
                order_kernel, [((FIRST + BLOCK, HALF), BF)] * GROUP, [((GROUP, FIRST, HALF), F32), ((6, BLOCK), F32)],
                *vectors_own, inputs.reshape(2 * CELLS, HALF), cotangent.reshape(2 * CELLS, HALF),
                joined_own, out_own, mib=ORDER_MIB,
            )
            v.slots = [slots[0]] + [turn(slots[s], s) for s in range(row_size - 1, 0, -1)][::-1]

        def stage_bias():
            labels = region_ids.reshape(2, WIN, 2, WIN).transpose(0, 2, 1, 3).reshape(GROUP, CELLS)
            (v.bias,) = step(
                bias_kernel, [((CELLS, STACK), F32)],
                [((24, REL), F32), ((WIN, 8, STRIP), F32), ((CELLS, CELLS), F32)],
                position_table.T, offset_index.T, labels, labels.T,
            )

        def stage_unpack():
            v.own, v.vectors, v.first = step(
                unpack_kernel, [(two, BF), ((8, WIDTH), F32), ((3, BLOCK, HALF), BF)], [],
                *v.slots, scalars=(slot_mask,),
            )
            v.first_other = swap(v.first)
            v.across = flip(v.own, 2)

        def stage_half():
            (half,) = step(half_kernel, [((BLOCK // 2, WIDTH), BF)], [], expand_weight)
            v.expand_mine = turn_all(half)

        def stage_stack():
            last.extend(v.tokens[1:] if STACK_TAKES else ())
            (v.expand,) = step(stack_kernel, [((3, BLOCK // 2, WIDTH), BF)], [], *v.expand_mine)
            v.expand_other = swap(v.expand)

        def stage_couple():
            (both,) = step(couple_kernel, [((2, *two), BF)], [], v.own, v.across)
            v.tokens = (both, flip(both, 1))

        def stage_first():
            v.joined_w, v.out_w = step(
                first_weights_kernel, [((3, WIDTH, BLOCK), BF), ((BLOCK, WIDTH), BF)],
                [((GROUP, 4, BLOCK // 2, HALF), BF)], joined_own, out_own, v.first, v.first_other,
            )

            v.out_across = flip(v.out_w, 2)

        def stage_couple_ow():
            (both,) = step(couple_out_kernel, [((2, BLOCK, WIDTH), BF)], [], v.out_w, v.out_across)
            v.out_square = (both, flip(both, 1))

        def stage_pass():
            (passed,) = step(pass_kernel, [((HALF, HALF), BF)], [], contract_own)
            v.contract = turn_all(passed)

        def stage_attend():
            v.x, v.n1, v.q, v.k, v.v, v.p, v.att = step(
                attend_kernel,
                [(wide, BF)] * 2 + [((TOKENS, BLOCK), BF)] * 3
                + [((GROUP, CELLS, STACK), BF), ((ATT, HALF), BF)],
                [((GROUP, STACK, BLOCK), BF), ((GROUP, BLOCK, CELLS), F32)], *v.tokens, v.vectors, v.joined_w, query_value_bias, v.bias,
            )
            v.att_across = flip(v.att, 2)

        def stage_expand_w():
            v.expand_w, v.hidden_bias = step(
                expand_weights_kernel, [((WIDTH, WIDTH), BF), ((1, WIDTH), F32)],
                [((GROUP, BLOCK, WIDTH), BF), ((8, WIDTH), F32)],
                expand_weight, v.expand, v.expand_other, expand_bias.reshape(1, WIDTH),
            )

        def stage_couple_att():
            (both,) = step(couple_att_kernel, [((2, ATT, HALF), BF)], [], v.att, v.att_across)
            v.attended = (both, flip(both, 1))

        def stage_expand():
            v.middle, v.n2, v.hidden, v.slope, *parts = step(
                expand_both_kernel, [(wide, F32), (wide, BF), (wide, BF), (wide, F32)] + [((HALF, HALF), BF)] * GROUP,
                [(wide, BF), ((WIDTH, WIDTH), BF), (wide, BF)],
                v.x, *v.attended, *v.out_square, v.vectors, v.expand_w, v.hidden_bias, *v.tokens,
            )
            v.parts_c = give_back(parts)

        def stage_contract_w():
            (v.contract_w,) = step(
                contract_weights_kernel, [((WIDTH, WIDTH), BF)], [], contract_own, *v.contract
            )

        def stage_hidden():
            v.up, v.pre, v.keep_n, send = step(
                hidden_back_kernel, [(wide, BF)] * 2 + [(two, F32), (two, BF)], [],
                *v.tokens, v.contract_w, v.slope, v.expand_w,
            )
            v.came_n = flip(send, 1)

        def stage_half_sum():
            (v.even,) = step(half_sum_kernel, [(two, BF)], [], v.keep_n, v.came_n)
            v.even_came = flip(v.even, 2)

        def stage_expand_g():
            v.keep_e, send_e, v.keep_out, send_out, v.hidden_sums = step(
                expand_grads_kernel,
                [((GROUP, BLOCK // 2, WIDTH), BF)] * 2 + [(two, F32), (two, BF), ((8, WIDTH), F32)],
                [((WIDTH, WIDTH), BF)],
                v.up, v.hidden, v.n2, v.pre, v.contract_w,
            )
            v.came_e = swap(send_e)
            v.came_out = flip(send_out, 1)

        def stage_cross():
            (v.even_total,) = step(cross_sum_kernel, [(two, BF)], [], v.even, v.even_came)
            v.odd_total = flip(v.even_total, 1)

        def stage_out_sum():
            (v.pair_out,) = step(half_sum_kernel, [(two, BF)], [], v.keep_out, v.came_out)
            v.far_out = flip(v.pair_out[CELLS:], 2)

        def stage_attend_b():
            v.own_mid, v.mid_low, v.joined_g, v.bias_g, v.keep_i, send = step(
                attend_back_kernel,
                [((CELLS, WIDTH), F32), (wide, BF), ((3, TOKENS, BLOCK), BF),
                 ((CELLS, STACK), F32), (more, F32), (more, BF)],
                [((TOKENS, BLOCK), BF), ((GROUP, STACK, BLOCK), BF), ((GROUP, STACK, BLOCK), BF),
                 ((GROUP, CELLS, STACK), BF), ((GROUP, BLOCK, CELLS), F32), ((16, WIDTH), F32)],
                v.even_total, v.odd_total, v.middle, v.up, v.vectors, v.out_w,
                v.q, v.k, v.v, v.p, v.joined_w, v.x, v.hidden_sums,
            )
            v.came_i = flip(send, 1)

        def stage_contract_s():
            (v.mine_c,) = step(
                ordered_sum_kernel, [((HALF, HALF), BF)], [((GROUP, HALF, HALF), BF)], *v.parts_c
            )

        def stage_expand_p():
            parts = step(
                expand_pack_kernel, [((BLOCK + EXTRA, HALF), BF)] * GROUP, [((GROUP, EXTRA, HALF), F32)],
                v.keep_e, v.came_e, v.middle, v.pair_out, v.far_out, v.vectors,
            )
            v.parts_e = give_back(parts)

        def stage_in_sum():
            (v.pair_in,) = step(input_sum_kernel, [(more, BF)], [], v.keep_i, v.came_i)
            v.far_in = flip(v.pair_in[CELLS:], 2)

        def stage_joined():
            v.keep_j, send = step(
                joined_grads_kernel, [((GROUP, rows_j, HALF), BF)] * 2,
                [((3, HALF, HALF), BF), ((GROUP, BLOCK // 2, HALF), BF),
                 ((GROUP, 2 * SMALL, HALF), F32), ((GROUP, 2 * SMALL, HALF), BF),
                 ((WIN, 8, STRIP), F32), ((HEADS, WIN, STRIP), F32)],
                v.n1, v.joined_g, v.att, v.mid_low, v.hidden_sums, v.bias_g, offset_index.T,
            )
            v.came_j = swap(send)

        def stage_expand_s():
            (mine,) = step(
                expand_sum_kernel, [((HALF + BLOCK, HALF), BF)], [((GROUP, BLOCK, HALF), BF)],
                v.mine_c, *v.parts_e,
            )
            v.mine_h = swap_rest(mine)
            v.other_h = swap(v.mine_h)

        def stage_joined_p():
            parts = step(
                joined_pack_kernel, [((rows_j + EXTRA, HALF), BF)] * GROUP, [((GROUP, EXTRA, HALF), F32)],
                v.keep_j, v.came_j, v.pair_in, v.far_in, v.x, v.own_mid, v.vectors,
            )
            v.parts_j = give_back(parts)

        def stage_restore():
            (v.layer_output,) = step(restore_kernel, [((2 * CELLS, HALF), BF)], [], *v.parts_e)

        def stage_finish_h():
            v.out_c, v.out_e = step(
                finish_hidden_kernel, [((HALF * 3, 128), F32), ((BLOCK, WIDTH), F32)], [],
                v.mine_h, v.other_h,
            )

        def stage_joined_s():
            (mine,) = step(
                joined_sum_kernel, [((rows_j + 16, HALF), BF)],
                [((GROUP, rows_j, HALF), BF), ((GROUP, 16, HALF), F32)], *v.parts_j
            )
            v.mine_j = swap_rest(mine)
            v.other_j = swap(v.mine_j)

        def stage_restore_w():
            (v.input_gradient,) = step(
                restore_wide_kernel, [((6 * CELLS, 128), F32)], [((2 * CELLS, HALF), F32)], *v.parts_j
            )

        def stage_finish_j():
            v.out_q, v.out_o, v.out_hidden, v.out_heads, v.out_table, *v.rows = step(
                finish_joined_kernel,
                [((BLOCK // 2 * 9, 128), F32), ((BLOCK // 2 * 3, 128), F32), ((6, 128), F32),
                 ((2, BLOCK), F32), ((HEADS, REL), F32)] + [((1, BLOCK), F32)] * 6,
                [((2 * SMALL, HALF), F32)],
                v.mine_j, v.other_j,
            )

        stage_order()
        stage_bias()
        stage_half()
        stage_unpack()
        stage_couple()
        stage_first()
        stage_pass()
        stage_stack()
        stage_attend()
        stage_couple_ow()
        stage_expand_w()
        stage_couple_att()
        stage_contract_w()
        stage_expand()
        stage_hidden()
        stage_half_sum()
        stage_expand_g()
        stage_cross()
        stage_out_sum()
        stage_attend_b()
        stage_contract_s()
        stage_expand_p()
        stage_joined()
        stage_in_sum()
        stage_expand_s()
        stage_joined_p()
        stage_restore()
        stage_finish_h()
        stage_joined_s()
        stage_restore_w()
        stage_finish_j()
        rows = [row.reshape(BLOCK) for row in v.rows]
        return (
            v.layer_output.reshape(inputs.shape),
            v.input_gradient.reshape(inputs.shape),
            rows[4],
            rows[5],
            v.out_q.reshape(query_key_value.shape),
            v.out_heads,
            v.out_table.T,
            v.out_o.reshape(output_weight.shape),
            rows[1],
            rows[2],
            rows[3],
            v.out_e,
            v.out_hidden.reshape(WIDTH),
            v.out_c.reshape(contract_weight.shape),
            rows[0],
        )

    return local


def solution(mesh):
    in_specs = (
        P(("dp", "col"), "row", None),
        P(("dp", "col"), "row", None),
        P(),
        P(),
        P(),
        P("row"),
        P("row"),
        P("row", None, "col", None),
        P(None, "col"),
        P(None, "col"),
        P("col", "row", None),
        P("row"),
        P("row"),
        P("row"),
        P("row", "col"),
        P("col"),
        P("col", "row", None),
        P("row"),
    )
    out_specs = (
        P(("dp", "col"), "row", None),
        P(("dp", "col"), "row", None),
        P("row"),
        P("row"),
        P("row", None, "col", None),
        P(None, "col"),
        P(None, "col"),
        P("col", "row", None),
        P("row"),
        P("row"),
        P("row"),
        P("row", "col"),
        P("col"),
        P("col", "row", None),
        P("row"),
    )
    local = local_program(mesh.shape["dp"], mesh.shape["row"], mesh.shape["col"])
    return jax.shard_map(local, mesh=mesh, in_specs=in_specs, out_specs=out_specs, check_vma=False)
```
